32 devices in a mesh: groups: 2 (over x), fsdp: 16 (over z, y, core).
Axes of the slice: x: 2, y: 2, z: 4, core: 2. Of those that a mesh axis runs over, the one named last changes fastest.
Arguments:
- hidden: bfloat16 [256, 8192], P('groups', 'fsdp'), parts along dimension 0
- parent_gain: float32 [16384], P('groups'), parts along dimension 0, may hold values from 0.1 to 1.9
- child_gain: float32 [16384], P('groups'), parts along dimension 0, may hold values from 0.1 to 1.9
- gate_weight: bfloat16 [4096, 8192], P(('groups', 'fsdp')), parts along dimension 0, may hold values from -0.0625 to 0.0625
- up_weight: bfloat16 [4096, 8192], P(('groups', 'fsdp')), parts along dimension 0, may hold values from -0.0625 to 0.0625
- down_weight: bfloat16 [4096, 8192], P(('groups', 'fsdp')), parts along dimension 0, may hold values from -0.125 to 0.125
- kept_index: int32 [4096], P('groups'), parts along dimension 0, may hold values from -1 to 2047, as said below
- tile_owner: int32 [32], P('groups'), parts along dimension 0, may hold values from 0 to 15, each once
Outputs:
- grad_gate: bfloat16 [4096, 8192], P(('groups', 'fsdp')), parts along dimension 0
- grad_up: bfloat16 [4096, 8192], P(('groups', 'fsdp')), parts along dimension 0
- grad_down: bfloat16 [4096, 8192], P(('groups', 'fsdp')), parts along dimension 0
- gain_grad: float32 [16384], P(('groups', 'fsdp')), parts along dimension 0
- loss_value: float32 [2], P('groups'), parts along dimension 0
The draws below stay inside these ranges and needn't reach their ends.
There are 2 independent parts, one for each index of `groups`. The reference program is written for one: setup_inputs(seed, part) draws one part's arguments, and reference() takes and returns one part's arrays. A program takes and returns all parts, laid end to end along the dimension named above; each array names one. Nothing has to cross between parts.
Inputs may be any that keep to these rules, and one draw needn't show every extreme that they name: `kept_index`: entry i is the parent channel placed in row i of the padded child, or -1 for an empty row; no channel appears twice; a tile takes at most 8 rows from the 128 channels of one device, and some tile has no empty row. `tile_owner`: each device along fsdp owns exactly one tile.
All inputs are finite; a program needn't handle non-finite values.
Results may differ from the reference program's by a relative error of at most 0.0045.
The reference program's roundings to bfloat16 on the way count: a program that leaves them out, or rounds other values in their place, can miss the bound.
Values may be sent and summed in bfloat16 or wider, within the bound.
No kernel may reach another device: no remote copies, remote signals or barrier semaphores. Data moves between devices by JAX's collectives and lax.ppermute only.
A program may use at most 128 MiB of HBM per device.

```python
import math
import jax
import jax.numpy as jnp
from jax import lax

D = 8192
TILE = 128
PC = 128
TOKENS = 128
FF_PAR = 2048
KEPT_ROWS = 2048
N_FSDP = 16


def draw_hidden(key, part):
    key = jax.random.fold_in(key, 11)
    key_base, key_col, key_row = jax.random.split(key, 3)
    base_vals = jax.random.truncated_normal(key_base, -4.0, 4.0, (TOKENS, D), jnp.float32)
    col_scale = jnp.exp(jax.random.uniform(key_col, (1, D), jnp.float32, math.log(0.3), math.log(3.5)))
    row_scale = jnp.exp(jax.random.uniform(key_row, (TOKENS, 1), jnp.float32, math.log(0.5), math.log(5.0)))
    return (base_vals * col_scale * row_scale).astype(jnp.bfloat16)


def draw_kept_index(key, part):
    key = jax.random.fold_in(key, 23)
    key_perm, key_level, key_coin, key_full, key_top, key_rows = jax.random.split(key, 6)
    sources = FF_PAR // PC
    tile_count = KEPT_ROWS // TILE
    per_pair = TILE // sources
    shuffles = jax.vmap(lambda subkey: jax.random.permutation(subkey, PC))(jax.random.split(key_perm, sources))
    channel = shuffles.reshape(sources, tile_count, per_pair) + (jnp.arange(sources) * PC)[:, None, None]
    keep_level = jax.random.randint(key_level, (sources,), 1, 5)
    top_parent = jax.random.randint(key_top, (), 0, sources)
    keep_level = jnp.where(jnp.arange(sources) == top_parent, 4, keep_level)
    coin_toss = jax.random.randint(key_coin, (sources, tile_count, per_pair), 0, 4)
    full_tile = jax.random.randint(key_full, (), 0, tile_count)
    is_live = (coin_toss < keep_level[:, None, None]) | (jnp.arange(tile_count)[None, :, None] == full_tile)
    entries = jnp.where(is_live, channel, -1)
    by_tile = jnp.transpose(entries, (1, 0, 2)).reshape(tile_count, TILE)
    row_order = jax.vmap(lambda subkey: jax.random.permutation(subkey, TILE))(jax.random.split(key_rows, tile_count))
    arranged = jnp.take_along_axis(by_tile, row_order, axis=1)
    return arranged.reshape(KEPT_ROWS).astype(jnp.int32)


def levels(key, dims, pieces, smallest, top_value):
    def one(dim, blocks):
        heights = jax.random.uniform(jax.random.fold_in(jax.random.fold_in(key, 6), dim), (blocks,), jnp.float32, smallest / len(pieces), top_value / len(pieces))
        return jnp.repeat(jnp.exp(heights), dims[dim] // blocks).reshape((-1,) + (1,) * (len(dims) - dim - 1))

    factor_of = one(*pieces[0])
    for cut in pieces[1:]:
        factor_of = factor_of * one(*cut)
    return factor_of


def bell_draw(key, dims, deviation, limit, cuts=(), kind=jnp.bfloat16):
    factor_of = levels(key, dims, cuts, -0.22, 0.18) if cuts else 1.0
    array = jax.random.normal(key, dims, jnp.float32) * deviation * factor_of
    return jnp.minimum(jnp.maximum(array, -limit), limit).astype(kind)


def setup_inputs(seed: int = 0, part: int = 0) -> dict:
    arg_keys = jax.random.split(jax.random.key(seed), 9)
    own_keys = jax.random.split(jax.random.fold_in(arg_keys[8], part), 9)
    return {
        "hidden": draw_hidden(jax.random.fold_in(jax.random.fold_in(arg_keys[8], part), 71), part),
        "parent_gain": jnp.clip(1.0 + 0.18 * jax.random.normal(own_keys[1], (D,), jnp.float32), 0.1, 1.9),
        "child_gain": jnp.clip(1.0 + 0.18 * jax.random.normal(own_keys[2], (D,), jnp.float32), 0.1, 1.9),
        "gate_weight": bell_draw(own_keys[3], (FF_PAR, D), D ** -0.5, 0.0625, ((0, 16),)),
        "up_weight": bell_draw(own_keys[4], (FF_PAR, D), D ** -0.5, 0.0625, ((0, 16),)),
        "down_weight": bell_draw(own_keys[5], (FF_PAR, D), FF_PAR ** -0.5, 0.125, ((0, 16),)),
        "kept_index": draw_kept_index(jax.random.fold_in(jax.random.fold_in(arg_keys[8], part), 71), part),
        "tile_owner": jax.random.permutation(own_keys[7], N_FSDP).astype(jnp.int32),
    }


def matmul(left_side, right_side):
    return jnp.dot(left_side, right_side, preferred_element_type=jnp.float32)

def select_rows(weights, safe_index, occupied):
    return jnp.where(occupied[:, None], weights[safe_index], jnp.zeros((), weights.dtype))

def place_tiles(grad_rows, tile_owner):
    tile_count = KEPT_ROWS // TILE
    grouped = grad_rows.reshape(tile_count, TILE, D)
    placed = jnp.zeros_like(grouped).at[tile_owner].set(grouped)
    return placed.reshape(KEPT_ROWS, D)

def reference(hidden, parent_gain, child_gain, gate_weight, up_weight, down_weight, kept_index, tile_owner):
    inputs_f = hidden.astype(jnp.float32)
    normed = inputs_f / jnp.sqrt(lax.optimization_barrier(jnp.mean(inputs_f * inputs_f, axis=1, keepdims=True)) + 1e-05)
    parent_in = (normed * parent_gain).astype(jnp.bfloat16)
    child_in = (normed * child_gain).astype(jnp.bfloat16)
    parent_gate = matmul(parent_in, gate_weight.T)
    parent_up = matmul(parent_in, up_weight.T)
    parent_hid = (parent_gate * jax.nn.sigmoid(parent_gate) * parent_up).astype(jnp.bfloat16)
    parent_out = matmul(parent_hid, down_weight)
    occupied = kept_index >= 0
    safe_index = jnp.where(occupied, kept_index, 0).astype(jnp.int32)
    child_gate_w = select_rows(gate_weight, safe_index, occupied)
    child_up_w = select_rows(up_weight, safe_index, occupied)
    child_down_w = select_rows(down_weight, safe_index, occupied)
    child_gate = matmul(child_in, child_gate_w.T)
    child_up = matmul(child_in, child_up_w.T)
    child_sig = jax.nn.sigmoid(child_gate)
    child_hid = (child_gate * child_sig * child_up).astype(jnp.bfloat16)
    difference = matmul(child_hid, child_down_w) - parent_out
    loss_value = (0.5 * jnp.sum(difference * difference) / (TOKENS * D)).reshape(1)
    out_slope = difference.astype(jnp.bfloat16)
    child_slope = matmul(out_slope, child_down_w.T)
    gate_back = (child_slope * child_up * child_sig * (1.0 + child_gate * (1.0 - child_sig))).astype(jnp.bfloat16)
    up_back = (child_slope * child_gate * child_sig).astype(jnp.bfloat16)
    down_rows = matmul(child_hid.T, out_slope).astype(jnp.bfloat16)
    gate_rows = matmul(gate_back.T, child_in).astype(jnp.bfloat16)
    up_rows = matmul(up_back.T, child_in).astype(jnp.bfloat16)
    grad_gate = place_tiles(gate_rows, tile_owner)
    grad_up = place_tiles(up_rows, tile_owner)
    grad_down = place_tiles(down_rows, tile_owner)
    input_slope = matmul(gate_back, child_gate_w) + matmul(up_back, child_up_w)
    gain_grad = lax.optimization_barrier(jnp.sum(input_slope * normed, axis=0))
    return (grad_gate, grad_up, grad_down, gain_grad, loss_value)
```

```python
import jax
import jax.numpy as jnp
from jax import lax
from jax.sharding import PartitionSpec as P


def matmul(left_side, right_side):
    return jnp.dot(left_side, right_side, preferred_element_type=jnp.float32)


def routing(kept_index, tile_owner, device, devices, parent_rows):
    tile_count = tile_owner.shape[0]
    tile_rows = kept_index.shape[0] // tile_count
    per_pair = tile_rows // devices
    layout = kept_index.reshape(tile_count, tile_rows)
    source = jnp.where(layout >= 0, layout // parent_rows, -1)
    from_each = (source[:, :, None] == jnp.arange(devices)[None, None, :]).astype(jnp.int32)
    earlier = jnp.cumsum(from_each, axis=1) - from_each
    position = jnp.sum(earlier * from_each, axis=2)
    local_row = layout - device * parent_rows
    picked = (source == device)[:, :, None] & (
        position[:, :, None] == jnp.arange(per_pair)[None, None, :]
    )
    chosen = jnp.sum(jnp.where(picked, local_row[:, :, None], 0), axis=1)
    present = jnp.any(picked, axis=1).astype(jnp.int32)
    owned_by = (tile_owner[None, :] == jnp.arange(devices)[:, None]).astype(jnp.int32)
    send_rows = jnp.sum(owned_by[:, :, None] * chosen[None, :, :], axis=1).reshape(-1)
    send_live = jnp.sum(owned_by[:, :, None] * present[None, :, :], axis=1).reshape(-1) > 0
    my_tile = jnp.sum(jnp.arange(tile_count) * (tile_owner == device).astype(jnp.int32))
    my_source = lax.dynamic_index_in_dim(source, my_tile, 0, keepdims=False)
    my_position = lax.dynamic_index_in_dim(position, my_tile, 0, keepdims=False)
    my_live = my_source >= 0
    recv_rows = jnp.where(my_live, my_source * per_pair + my_position, 0)
    return (send_rows, send_live, recv_rows, my_live)


def select_rows(row_of_slot, live, back):
    hot = (row_of_slot[:, None] == jnp.arange(back.shape[1])[None, :]) & live[:, None]
    return lax.dot_general(
        hot.astype(jnp.bfloat16), back, (((1,), (1,)), ((), ())), preferred_element_type=jnp.float32
    ).astype(jnp.bfloat16)


def place_rows(slot_of_row, live, received):
    hot = (slot_of_row[:, None] == jnp.arange(received.shape[0])[None, :]) & live[:, None]
    return matmul(hot.astype(jnp.bfloat16), received).astype(jnp.bfloat16)


def shards(
    hidden, parent_gain, child_gain, gate_weight, up_weight, down_weight, kept_index, tile_owner
):
    devices = lax.axis_size("fsdp")
    device = lax.axis_index("fsdp")
    parent_rows = gate_weight.shape[0]
    full_rows = lax.all_gather(hidden, "fsdp", axis=1, tiled=True)
    token_count = full_rows.shape[0]
    feat_width = full_rows.shape[1]
    inputs_f = full_rows.astype(jnp.float32)
    normed = inputs_f / jnp.sqrt(jnp.mean(inputs_f * inputs_f, axis=1, keepdims=True) + 1e-05)
    parent_in = (normed * parent_gain).astype(jnp.bfloat16)
    child_in = (normed * child_gain).astype(jnp.bfloat16)
    send_rows, send_live, recv_rows, my_live = routing(
        kept_index, tile_owner, device, devices, parent_rows
    )
    kept_here = jnp.any(
        send_live[:, None] & (send_rows[:, None] == jnp.arange(parent_rows)[None, :]), axis=0
    )
    both_in = jnp.concatenate([parent_in, child_in], axis=0)
    gate_both = matmul(both_in, gate_weight.T)
    up_both = matmul(both_in, up_weight.T)
    parent_gate = gate_both[:token_count]
    parent_up = up_both[:token_count]
    child_gate = gate_both[token_count:]
    child_up = up_both[token_count:]
    parent_hid = (parent_gate * jax.nn.sigmoid(parent_gate) * parent_up).astype(jnp.bfloat16)
    child_sig = jax.nn.sigmoid(child_gate)
    child_hid = jnp.where(kept_here[None, :], child_gate * child_sig * child_up, 0.0).astype(
        jnp.bfloat16
    )
    hid_sent = select_rows(send_rows, send_live, child_hid).reshape(devices, -1, token_count)
    hid_sent = lax.all_to_all(hid_sent, "fsdp", split_axis=0, concat_axis=0, tiled=True)
    hid_tile = place_rows(recv_rows, my_live, hid_sent.reshape(-1, token_count))
    difference = lax.psum(matmul(child_hid, down_weight) - matmul(parent_hid, down_weight), "fsdp")
    loss_value = 0.5 * jnp.sum(difference * difference) / (token_count * feat_width)
    out_slope = difference.astype(jnp.bfloat16)
    child_slope = matmul(out_slope, down_weight.T)
    gate_back = child_slope * child_up * child_sig * (1.0 + child_gate * (1.0 - child_sig))
    up_back = child_slope * child_gate * child_sig
    gate_back = jnp.where(kept_here[None, :], gate_back, 0.0).astype(jnp.bfloat16)
    up_back = jnp.where(kept_here[None, :], up_back, 0.0).astype(jnp.bfloat16)
    input_slope = matmul(gate_back, gate_weight) + matmul(up_back, up_weight)
    gain_part = jnp.sum(input_slope * normed, axis=0)
    gain_grad = lax.psum_scatter(gain_part, "fsdp", scatter_dimension=0, tiled=True)
    per_pair = send_rows.shape[0] // devices
    both = jnp.stack(
        [
            select_rows(send_rows, send_live, gate_back).reshape(devices, per_pair, token_count),
            select_rows(send_rows, send_live, up_back).reshape(devices, per_pair, token_count),
        ],
        axis=1,
    )
    both = lax.all_to_all(both, "fsdp", split_axis=0, concat_axis=0, tiled=True)
    gate_tile = place_rows(recv_rows, my_live, both[:, 0].reshape(-1, token_count))
    up_tile = place_rows(recv_rows, my_live, both[:, 1].reshape(-1, token_count))
    grad_gate = matmul(gate_tile, child_in).astype(jnp.bfloat16)
    grad_up = matmul(up_tile, child_in).astype(jnp.bfloat16)
    grad_down = matmul(hid_tile, out_slope).astype(jnp.bfloat16)
    return (grad_gate, grad_up, grad_down, gain_grad, loss_value.reshape(1))


def solution(mesh):
    placed = (
        P("groups", "fsdp"),
        P("groups"),
        P("groups"),
        P(("groups", "fsdp"), None),
        P(("groups", "fsdp"), None),
        P(("groups", "fsdp"), None),
        P("groups"),
        P("groups"),
    )
    return jax.shard_map(
        shards,
        mesh=mesh,
        in_specs=placed,
        out_specs=(
            P(("groups", "fsdp"), None),
            P(("groups", "fsdp"), None),
            P(("groups", "fsdp"), None),
            P(("groups", "fsdp")),
            P("groups"),
        ),
        check_vma=False,
    )
```

```python
import functools

import jax
import jax.numpy as jnp
from jax import lax
from jax.experimental import pallas as pl
from jax.experimental.pallas import tpu as pltpu
from jax.sharding import PartitionSpec as P

BF16 = jnp.bfloat16
F32 = jnp.float32
NT = (((1,), (1,)), ((), ()))


def dot(left, right):
    return jnp.dot(left, right, preferred_element_type=F32)


def dot_nt(left, right):
    return lax.dot_general(left, right, NT, preferred_element_type=F32)


class Ring:
    def __init__(self, devices):
        self.chips = devices // 2
        self.snake = self.chips == 8
        self.devices = devices
        self.up_steps = self.chips // 2
        self.down_steps = self.chips - 1 - self.up_steps
        self.sibling = [(i, i ^ 1) for i in range(devices)]

    def chip_at(self, place):
        if not self.snake:
            return place
        return jnp.where(
            place < self.chips // 2, 2 * place, 2 * (self.chips - 1 - place) + 1
        )

    def place_of(self, chip):
        if not self.snake:
            return chip
        return jnp.where(chip % 2 == 0, chip // 2, self.chips - 1 - chip // 2)

    def owner(self, device, distance, core):
        chip = self.chip_at((self.place_of(device // 2) + distance) % self.chips)
        return 2 * chip + (device % 2 + core) % 2

    def shift(self, step):
        pairs = []
        for i in range(self.devices):
            place = i // 2
            if self.snake:
                place = i // 4 if place % 2 == 0 else self.chips - 1 - place // 2
            place = (place + step) % self.chips
            chip = place
            if self.snake:
                half = self.chips // 2
                chip = 2 * place if place < half else 2 * (self.chips - 1 - place) + 1
            pairs.append((i, 2 * chip + i % 2))
        return pairs

    def gather(self, block, device):
        tokens, width = block.shape
        whole = jnp.zeros((tokens, width * self.devices), block.dtype)

        def put(whole, part, distance, core):
            owner = self.owner(device, distance, core)
            return lax.dynamic_update_slice(whole, part, (0, owner * width))

        whole = put(whole, block, 0, 0)
        whole = put(whole, lax.ppermute(block, "fsdp", self.sibling), 0, 1)
        up = down = block
        for step in range(1, self.up_steps + 1):
            both = step <= self.down_steps
            up = lax.ppermute(up, "fsdp", self.shift(1))
            if both:
                down = lax.ppermute(down, "fsdp", self.shift(-1))
            whole = put(whole, up, self.chips - step, 0)
            whole = put(whole, lax.ppermute(up, "fsdp", self.sibling), self.chips - step, 1)
            if both:
                whole = put(whole, down, step, 0)
                whole = put(whole, lax.ppermute(down, "fsdp", self.sibling), step, 1)
        return whole

    def scatter_sum(self, term):
        up = term(self.up_steps)
        down = term(self.up_steps + 1) if self.down_steps else None
        for step in range(1, self.up_steps + 1):
            up = lax.ppermute(up.astype(BF16), "fsdp", self.shift(1)).astype(F32)
            if step <= self.down_steps:
                down = lax.ppermute(down.astype(BF16), "fsdp", self.shift(-1)).astype(F32)
            if step < self.up_steps:
                up = up + term(self.up_steps - step)
            if step < self.down_steps:
                down = down + term(self.up_steps + 1 + step)
        total = term(0) + up
        return total + down if self.down_steps else total


def routing(kept_index, tile_owner, device, devices, parent_rows):
    tile_count = tile_owner.shape[0]
    tile_rows = kept_index.shape[0] // tile_count
    per_pair = tile_rows // devices
    kinds = 3
    slots = devices * kinds * per_pair
    layout = kept_index.reshape(tile_count, tile_rows)
    local = layout - device * parent_rows
    mine = (local >= 0) & (local < parent_rows)
    earlier = jnp.arange(tile_rows)[:, None] < jnp.arange(tile_rows)[None, :]
    position = dot(mine.astype(BF16), earlier.astype(BF16)).astype(jnp.int32)
    slot = jnp.where(mine, tile_owner[:, None] * (kinds * per_pair) + position, -1).reshape(-1)
    at_slot = (slot[None, :] == jnp.arange(slots)[:, None]).astype(BF16)
    at_row = (local.reshape(-1)[:, None] == jnp.arange(parent_rows)[None, :]).astype(BF16)
    send = dot(at_slot, at_row).astype(BF16)
    kept = jnp.any(local.reshape(-1)[:, None] == jnp.arange(parent_rows)[None, :], axis=0)
    mine_row = jnp.sum(jnp.where((tile_owner == device)[:, None], layout, 0), axis=0)
    source = jnp.where(mine_row >= 0, mine_row // parent_rows, -1)
    same = (source[:, None] == source[None, :]) & earlier.T
    rank = jnp.sum(same.astype(jnp.int32), axis=1)
    from_slot = jnp.where(mine_row >= 0, source * (kinds * per_pair) + rank, -slots)
    place = (from_slot[:, None] == jnp.arange(slots)[None, :]).astype(BF16)
    return send, place, kept.astype(F32).reshape(1, parent_rows), per_pair


def forward_kernel(
    ring,
    hidden,
    parent_gain,
    child_gain,
    gate,
    up,
    down,
    kept,
    child_in,
    scale,
    child_gate,
    child_up,
    child_hid,
    keep,
    send,
):
    tokens, features = hidden.shape
    width = features // ring.devices
    pieces = 16
    piece = features // pieces
    cuts = [slice(k * piece, (k + 1) * piece) for k in range(pieces)]
    squares = jnp.zeros((tokens, piece), F32)
    for cols in cuts:
        h = hidden[:, cols].astype(F32)
        squares = squares + h * h
    mean = jnp.sum(squares, axis=1, keepdims=True) / features
    inverse = 1.0 / jnp.sqrt(mean + 1e-05)
    scale[...] = jnp.broadcast_to(inverse, scale.shape)
    gate_both = jnp.zeros((2 * tokens, gate.shape[0]), F32)
    up_both = jnp.zeros((2 * tokens, gate.shape[0]), F32)
    for cols in cuts:
        normed = hidden[:, cols].astype(F32) * inverse
        parent = (normed * parent_gain[:, cols]).astype(BF16)
        child = (normed * child_gain[:, cols]).astype(BF16)
        child_in[:, cols] = child
        both = jnp.concatenate([parent, child], axis=0)
        gate_both = gate_both + dot_nt(both, gate[:, cols])
        up_both = up_both + dot_nt(both, up[:, cols])
    hid = gate_both * jax.nn.sigmoid(gate_both) * up_both
    child_gate[...] = gate_both[tokens:]
    child_up[...] = up_both[tokens:]
    child = jnp.where(kept[...] > 0, hid[tokens:], 0.0).astype(BF16)
    child_hid[...] = child
    both_hid = jnp.concatenate([child, -hid[:tokens].astype(BF16)], axis=0)
    device = lax.axis_index("fsdp")
    for core, target in ((1, send), (0, keep)):
        for distance in range(ring.chips):
            start = ring.owner(device, distance, core) * width
            out = dot(both_hid, down[:, pl.ds(pl.multiple_of(start, width), width)])
            target[distance] = out[:tokens] + out[tokens:]


def slope_kernel(
    slope, down, kept, child_gate, child_up, child_hid, select, gate_back, up_back, sent
):
    child_slope = dot_nt(slope[...], down[...])
    g, u = child_gate[...], child_up[...]
    sig = jax.nn.sigmoid(g)
    live = kept[...] > 0
    for_gate = child_slope * u * sig * (1.0 + g * (1.0 - sig))
    for_gate = jnp.where(live, for_gate, 0.0).astype(BF16)
    for_up = jnp.where(live, child_slope * g * sig, 0.0).astype(BF16)
    gate_back[...] = for_gate
    up_back[...] = for_up
    sent[...] = (
        dot_nt(select[0], for_gate) + dot_nt(select[1], for_up) + dot_nt(select[2], child_hid[...])
    ).astype(BF16)


def gain_kernel(gate_back, up_back, gate, up, hidden, scale, difference, lanes):
    devices, rows, _ = lanes.shape
    width = hidden.shape[1] // devices
    inverse = scale[...][:, :1]
    loss = jnp.sum(difference[...] * difference[...], axis=0, keepdims=True)
    loss = jnp.broadcast_to(jnp.sum(loss, axis=1, keepdims=True), (1, 128))
    for k in range(devices):
        cols = slice(k * width, (k + 1) * width)
        input_slope = dot(gate_back[...], gate[:, cols]) + dot(up_back[...], up[:, cols])
        normed = hidden[:, cols].astype(F32) * inverse
        part = jnp.sum(input_slope * normed, axis=0, keepdims=True)
        for r in range(width // 128):
            lanes[k, r : r + 1, :] = part[:, r * 128 : (r + 1) * 128]
        lanes[k, width // 128 : width // 128 + 1, :] = loss


def rows_kernel(received, place, child_in, slope, grad_gate, grad_up, grad_down, tiles):
    rows = grad_gate.shape[0]

    @pl.when(pl.program_id(0) == 0)
    def _():
        for kind in range(3):
            tiles[kind * rows : (kind + 1) * rows, :] = dot(place[kind], received[...]).astype(BF16)

    out = dot(tiles[: 2 * rows, :], child_in[...]).astype(BF16)
    grad_gate[...] = out[:rows]
    grad_up[...] = out[rows:]
    grad_down[...] = dot(tiles[2 * rows :, :], slope[...]).astype(BF16)


VMEM = pl.BlockSpec(memory_space=pltpu.VMEM)
MIB = 1024 * 1024


def call(kernel, outs, operands, limit, name):
    return pl.pallas_call(
        kernel,
        out_shape=[jax.ShapeDtypeStruct(shape, dtype) for shape, dtype in outs],
        in_specs=[VMEM] * len(operands),
        out_specs=[VMEM] * len(outs),
        compiler_params=pltpu.CompilerParams(vmem_limit_bytes=limit * MIB),
        name=name,
    )(*operands)


def shards(
    hidden, parent_gain, child_gain, gate_weight, up_weight, down_weight, kept_index, tile_owner
):
    devices = lax.axis_size("fsdp")
    device = lax.axis_index("fsdp")
    ring = Ring(devices)
    chips = ring.chips
    parent_rows = gate_weight.shape[0]
    tokens, width = hidden.shape
    features = width * devices
    send, place, kept, per_pair = routing(kept_index, tile_owner, device, devices, parent_rows)
    select = jnp.stack([jnp.roll(send, kind * per_pair, axis=0) for kind in range(3)])
    places = jnp.stack([jnp.roll(place, kind * per_pair, axis=1) for kind in range(3)])

    square = ((tokens, parent_rows), F32)
    wide = ((tokens, features), BF16)
    hidden_all = ring.gather(hidden, device)
    child_in, scale, child_gate, child_up, child_hid, keep, other = call(
        functools.partial(forward_kernel, ring),
        [
            wide,
            ((tokens, 128), F32),
            square,
            square,
            ((tokens, parent_rows), BF16),
            ((chips, tokens, width), F32),
            ((chips, tokens, width), F32),
        ],
        [
            hidden_all,
            parent_gain.reshape(1, features),
            child_gain.reshape(1, features),
            gate_weight,
            up_weight,
            down_weight,
            kept,
        ],
        limit=20,
        name="forward",
    )
    first = list(range(ring.up_steps, min(ring.up_steps + 2, chips)))
    rest = [j for j in range(chips) if j not in first]
    swapped = {}
    lead = lax.ppermute(other[first[0] : first[-1] + 1], "fsdp", ring.sibling)
    for i, j in enumerate(first):
        swapped[j] = lead[i]
    for run in ([j for j in rest if j < first[0]], [j for j in rest if j > first[-1]]):
        if run:
            part = lax.ppermute(other[run[0] : run[-1] + 1], "fsdp", ring.sibling)
            for i, j in enumerate(run):
                swapped[j] = part[i]
    difference = ring.scatter_sum(lambda j: keep[j] + swapped[j])
    slope_all = ring.gather(difference.astype(BF16), device)

    slots = send.shape[0]
    gate_back, up_back, sent = call(
        slope_kernel,
        [((tokens, parent_rows), BF16), ((tokens, parent_rows), BF16), ((slots, tokens), BF16)],
        [slope_all, down_weight, kept, child_gate, child_up, child_hid, select],
        limit=8,
        name="slope",
    )
    received = lax.all_to_all(
        sent.reshape(devices, slots // devices, tokens), "fsdp", 0, 0, tiled=True
    ).reshape(slots, tokens)
    gain_rows = width // 128
    (lanes,) = call(
        gain_kernel,
        [((devices, -(-(gain_rows + 1) // 8) * 8, 128), F32)],
        [gate_back, up_back, gate_weight, up_weight, hidden_all, scale, difference],
        limit=8,
        name="gain",
    )
    received, lanes = lax.optimization_barrier((received, lanes))
    lanes = jnp.sum(lax.all_to_all(lanes, "fsdp", 0, 0, tiled=True), axis=0)
    gain_grad = lanes[:gain_rows].reshape(width)
    loss_value = 0.5 * lanes[gain_rows, :1] / (tokens * features)

    cut = min(features, 1024)
    column = pl.BlockSpec((tokens, cut), lambda i: (0, i))
    grad = pl.BlockSpec((parent_rows, cut), lambda i: (0, i))
    grad_gate, grad_up, grad_down = pl.pallas_call(
        rows_kernel,
        out_shape=[jax.ShapeDtypeStruct((parent_rows, features), BF16)] * 3,
        grid=(features // cut,),
        in_specs=[
            pl.BlockSpec((slots, tokens), lambda i: (0, 0)),
            pl.BlockSpec(places.shape, lambda i: (0, 0, 0)),
            column,
            column,
        ],
        out_specs=[grad] * 3,
        scratch_shapes=[pltpu.VMEM((3 * parent_rows, tokens), BF16)],
        compiler_params=pltpu.CompilerParams(vmem_limit_bytes=8 * MIB),
        name="rows",
    )(received, places, child_in, slope_all)
    return (grad_gate, grad_up, grad_down, gain_grad, loss_value)


def solution(mesh):
    placed = (
        P("groups", "fsdp"),
        P("groups"),
        P("groups"),
        P(("groups", "fsdp"), None),
        P(("groups", "fsdp"), None),
        P(("groups", "fsdp"), None),
        P("groups"),
        P("groups"),
    )
    return jax.shard_map(
        shards,
        mesh=mesh,
        in_specs=placed,
        out_specs=(
            P(("groups", "fsdp"), None),
            P(("groups", "fsdp"), None),
            P(("groups", "fsdp"), None),
            P(("groups", "fsdp")),
            P("groups"),
        ),
        check_vma=False,
    )
```

```python
import functools

import jax
import jax.numpy as jnp
from jax import lax
from jax.experimental import pallas as pl
from jax.experimental.pallas import tpu as pltpu
from jax.sharding import PartitionSpec as P

BF16 = jnp.bfloat16
F32 = jnp.float32
NT = (((1,), (1,)), ((), ()))


def dot(left, right):
    return jnp.dot(left, right, preferred_element_type=F32)


def dot_nt(left, right):
    return lax.dot_general(left, right, NT, preferred_element_type=F32)


def after(value, other):
    return lax.optimization_barrier((value, other))[0]


def place(whole, part, owner):
    return lax.dynamic_update_slice(whole, part, (0, owner * part.shape[1]))


class Ring:
    def __init__(self, devices):
        self.devices = devices
        self.chips = devices // 2
        self.up_steps = self.chips // 2
        self.down_steps = self.chips - 1 - self.up_steps
        self.sibling = [(i, i ^ 1) for i in range(devices)]

    def owner(self, device, distance, core):
        return 2 * ((device // 2 + distance) % self.chips) + (device % 2 + core) % 2

    def shift(self, step):
        return [(i, (i + 2 * step) % self.devices) for i in range(self.devices)]

    def gather(self, block, device):
        tokens, width = block.shape
        whole = jnp.zeros((tokens, width * self.devices), block.dtype)

        def put(whole, part, distance):
            whole = place(whole, part, self.owner(device, distance, 0))
            other = lax.ppermute(part, "fsdp", self.sibling)
            return place(whole, other, self.owner(device, distance, 1))

        whole = put(whole, block, 0)
        up = down = block
        for step in range(1, self.up_steps + 1):
            up = lax.ppermute(up, "fsdp", self.shift(1))
            if step <= self.down_steps:
                down = lax.ppermute(down, "fsdp", self.shift(-1))
            whole = put(whole, up, self.chips - step)
            if step <= self.down_steps:
                whole = put(whole, down, step)
        return whole

    def scatter_sum(self, keep, other):
        swapped = lax.ppermute(other, "fsdp", self.sibling)

        def term(distance):
            return keep[distance] + swapped[distance]

        up = term(self.up_steps)
        down = term(self.up_steps + 1) if self.down_steps else None
        for step in range(1, self.up_steps + 1):
            up = lax.ppermute(up.astype(BF16), "fsdp", self.shift(1)).astype(F32)
            if step <= self.down_steps:
                down = lax.ppermute(down.astype(BF16), "fsdp", self.shift(-1)).astype(F32)
            if step < self.up_steps:
                up = up + term(self.up_steps - step)
            if step < self.down_steps:
                down = down + term(self.up_steps + 1 + step)
        total = term(0) + up
        return total + down if self.down_steps else total


class Grid(Ring):
    FAR_FIRST = (3, 2, 1, 0)

    def across(self, bits):
        return [(i, i ^ bits) for i in range(self.devices)]

    def owner(self, device, distance, core):
        return jnp.bitwise_xor(device, 2 * distance + core)

    def gather(self, block, device):
        tokens, width = block.shape
        whole = jnp.zeros((tokens, width * self.devices), block.dtype)
        column = {0: block}
        for z in (1, 2):
            column[z] = lax.ppermute(block, "fsdp", self.across(4 * z))
        column[3] = lax.ppermute(after(block, column[1]), "fsdp", self.across(12))
        for z in range(4):
            for y in range(2):
                part = lax.ppermute(column[z], "fsdp", self.across(2)) if y else column[z]
                whole = place(whole, part, self.owner(device, 2 * z + y, 0))
                part = lax.ppermute(part, "fsdp", self.sibling)
                whole = place(whole, part, self.owner(device, 2 * z + y, 1))
        return whole

    def scatter_sum(self, keep, other):
        over_y = {}
        mine = {}
        sent = None
        for z in self.FAR_FIRST:
            pair = slice(2 * z, 2 * z + 2)
            part = lax.ppermute(other[pair], "fsdp", self.sibling)
            if sent is not None:
                part = after(part, sent)
            part = keep[pair] + part
            sent = part[1].astype(BF16)
            mine[z] = part[0]
            over_y[z] = lax.ppermute(sent, "fsdp", self.across(2))
        arrived = []
        sent = None
        for z in self.FAR_FIRST:
            part = over_y[z] if sent is None else after(over_y[z], sent)
            total = mine[z] + part.astype(F32)
            if z:
                sent = total.astype(BF16)
                arrived.append(lax.ppermute(sent, "fsdp", self.across(4 * z)))
        for part in arrived:
            total = total + part.astype(F32)
        return total


def kept_rows(kept_index, device, parent_rows):
    local = kept_index[:, None] - device * parent_rows
    kept = jnp.any(local == jnp.arange(parent_rows)[None, :], axis=0)
    return kept.astype(F32).reshape(1, parent_rows)


def routing(kept_index, tile_owner, device, devices, parent_rows, stride):
    tile_count = tile_owner.shape[0]
    tile_rows = kept_index.shape[0] // tile_count
    slots = devices * stride
    layout = kept_index.reshape(tile_count, tile_rows)
    local = layout - device * parent_rows
    mine = (local >= 0) & (local < parent_rows)
    earlier = jnp.arange(tile_rows)[:, None] < jnp.arange(tile_rows)[None, :]
    position = dot(mine.astype(BF16), earlier.astype(BF16)).astype(jnp.int32)
    slot = jnp.where(mine, tile_owner[:, None] * stride + position, -1).reshape(-1)
    at_slot = (slot[None, :] == jnp.arange(slots)[:, None]).astype(BF16)
    at_row = (local.reshape(-1)[:, None] == jnp.arange(parent_rows)[None, :]).astype(BF16)
    send = dot(at_slot, at_row).astype(BF16)
    tile = jnp.sum(jnp.where((tile_owner == device)[:, None], layout, 0), axis=0)
    source = jnp.where(tile >= 0, tile // parent_rows, -1)
    same = (source[:, None] == source[None, :]) & earlier.T
    rank = jnp.sum(same.astype(jnp.int32), axis=1)
    slot = jnp.where(tile >= 0, source * stride + rank, -slots)
    find = (slot[:, None] == jnp.arange(slots)[None, :]).astype(BF16)
    return send, find


def forward_kernel(
    ring,
    hidden,
    parent_gain,
    child_gain,
    gate,
    up,
    down,
    kept,
    scale,
    child_gate,
    child_up,
    child_hid,
    keep,
    send,
):
    tokens, features = hidden.shape
    width = features // ring.devices
    pieces = 16
    piece = features // pieces
    cuts = [slice(k * piece, (k + 1) * piece) for k in range(pieces)]
    squares = jnp.zeros((tokens, piece), F32)
    for cols in cuts:
        h = hidden[:, cols].astype(F32)
        squares = squares + h * h
    mean = jnp.sum(squares, axis=1, keepdims=True) / features
    inverse = 1.0 / jnp.sqrt(mean + 1e-05)
    scale[...] = jnp.broadcast_to(inverse, scale.shape)
    gate_both = jnp.zeros((2 * tokens, gate.shape[0]), F32)
    up_both = jnp.zeros((2 * tokens, gate.shape[0]), F32)
    for cols in cuts:
        normed = hidden[:, cols].astype(F32) * inverse
        parent = (normed * parent_gain[:, cols]).astype(BF16)
        child = (normed * child_gain[:, cols]).astype(BF16)
        both = jnp.concatenate([parent, child], axis=0)
        gate_both = gate_both + dot_nt(both, gate[:, cols])
        up_both = up_both + dot_nt(both, up[:, cols])
    hid = gate_both * jax.nn.sigmoid(gate_both) * up_both
    child_gate[...] = gate_both[tokens:]
    child_up[...] = up_both[tokens:]
    child = jnp.where(kept[...] > 0, hid[tokens:], 0.0).astype(BF16)
    child_hid[...] = child
    both_hid = jnp.concatenate([child, -hid[:tokens].astype(BF16)], axis=0)
    device = lax.axis_index("fsdp")
    for core, target in ((1, send), (0, keep)):
        for distance in range(ring.chips):
            start = ring.owner(device, distance, core) * width
            out = dot(both_hid, down[:, pl.ds(pl.multiple_of(start, width), width)])
            target[distance] = out[:tokens] + out[tokens:]


def backward_kernel(
    per_pair,
    slope,
    hidden,
    gate,
    up,
    down,
    kept,
    scale,
    child_gate,
    child_up,
    child_hid,
    select,
    sent,
    message,
):
    devices, stride, _ = message.shape
    tokens = slope.shape[0]
    width = slope.shape[1] // devices
    child_slope = dot_nt(slope[...], down[...])
    g, u = child_gate[...], child_up[...]
    sig = jax.nn.sigmoid(g)
    live = kept[...] > 0
    gate_back = child_slope * u * sig * (1.0 + g * (1.0 - sig))
    gate_back = jnp.where(live, gate_back, 0.0).astype(BF16)
    up_back = jnp.where(live, child_slope * g * sig, 0.0).astype(BF16)
    rows = dot_nt(select[0], gate_back) + dot_nt(select[1], up_back)
    rows = rows + dot_nt(select[2], child_hid[...])
    message[...] = rows.reshape(devices, stride, tokens)
    inverse = scale[...][:, :1]
    high_at, gain_rows = 3 * per_pair, width // 128
    for k in range(devices):
        cols = slice(k * width, (k + 1) * width)
        input_slope = dot(gate_back, gate[:, cols]) + dot(up_back, up[:, cols])
        normed = hidden[:, cols].astype(F32) * inverse
        part = jnp.sum(input_slope * normed, axis=0, keepdims=True)
        high = part.astype(BF16).astype(F32)
        for r in range(gain_rows):
            lanes = slice(r * 128, (r + 1) * 128)
            at = high_at + r
            message[k, at : at + 1, :] = high[:, lanes]
            at = at + gain_rows
            message[k, at : at + 1, :] = (part - high)[:, lanes]
    sent[...] = message[...].astype(BF16)


def rows_kernel(
    per_pair,
    received,
    places,
    hidden,
    scale,
    child_gain,
    slope,
    grad_gate,
    grad_up,
    grad_down,
    gain,
    loss,
    made,
    done,
):
    rows, features = grad_gate.shape
    devices, stride, tokens = received.shape
    message = received[...].reshape(devices * stride, tokens)
    tiles = [dot(places[kind], message).astype(BF16) for kind in range(3)]
    both = jnp.concatenate(tiles[:2], axis=0)
    inverse = scale[...][:, :1]
    cut = min(features, 1024)
    copies = []
    squares = jnp.zeros((slope.shape[0], cut), F32)
    for k in range(features // cut):
        cols = slice(k * cut, (k + 1) * cut)
        difference = slope[:, cols]
        squares = squares + difference.astype(F32) * difference.astype(F32)
        made[2, :, cols] = dot(tiles[2], difference).astype(BF16)
        child = (hidden[:, cols].astype(F32) * inverse * child_gain[:, cols]).astype(BF16)
        out = dot(both, child).astype(BF16)
        made[0, :, cols] = out[:rows]
        made[1, :, cols] = out[rows:]
        for kind, grad in enumerate((grad_gate, grad_up, grad_down)):
            copy = pltpu.make_async_copy(made.at[kind, :, cols], grad.at[:, cols], done.at[kind, k])
            copy.start()
            copies.append(copy)
    squares = jnp.sum(jnp.sum(squares, axis=0, keepdims=True), axis=1, keepdims=True)
    loss[...] = 0.5 * squares / (slope.shape[0] * features)
    total = jnp.sum(message.astype(F32).reshape(devices, stride, tokens), axis=0)
    gain_rows = gain.shape[1] // 128
    for r in range(gain_rows):
        at = 3 * per_pair + r
        gain[:, r * 128 : (r + 1) * 128] = (
            total[at : at + 1, :] + total[at + gain_rows : at + gain_rows + 1, :]
        )
    for copy in copies:
        copy.wait()


VMEM = pl.BlockSpec(memory_space=pltpu.VMEM)
MIB = 1024 * 1024


def call(kernel, outs, operands, limit, name, scratch=(), specs=None):
    return pl.pallas_call(
        kernel,
        out_shape=[jax.ShapeDtypeStruct(shape, dtype) for shape, dtype in outs],
        in_specs=[VMEM] * len(operands),
        out_specs=specs or [VMEM] * len(outs),
        scratch_shapes=list(scratch),
        compiler_params=pltpu.CompilerParams(vmem_limit_bytes=limit * MIB),
        name=name,
    )(*operands)


def shards(
    hidden, parent_gain, child_gain, gate_weight, up_weight, down_weight, kept_index, tile_owner
):
    devices = lax.axis_size("fsdp")
    device = lax.axis_index("fsdp")
    ring = Grid(devices) if devices == 16 else Ring(devices)
    chips = ring.chips
    parent_rows = gate_weight.shape[0]
    tokens, width = hidden.shape
    features = width * devices
    per_pair = kept_index.shape[0] // tile_owner.shape[0] // devices
    stride = -(-(3 * per_pair + 2 * (width // 128)) // 8) * 8
    kept = kept_rows(kept_index, device, parent_rows)

    square = ((tokens, parent_rows), F32)
    gains = [parent_gain.reshape(1, features), child_gain.reshape(1, features)]
    hidden_all = ring.gather(hidden, device)
    scale, child_gate, child_up, child_hid, keep, other = call(
        functools.partial(forward_kernel, ring),
        [
            ((tokens, 128), F32),
            square,
            square,
            ((tokens, parent_rows), BF16),
            ((chips, tokens, width), F32),
            ((chips, tokens, width), F32),
        ],
        [
            hidden_all,
            *gains,
            gate_weight,
            up_weight,
            down_weight,
            kept,
        ],
        limit=12,
        name="forward",
    )
    difference = ring.scatter_sum(keep, other)
    slope_all = ring.gather(difference.astype(BF16), device)

    send, find = routing(
        after(kept_index, child_hid), tile_owner, device, devices, parent_rows, stride
    )
    select = jnp.stack([jnp.roll(send, kind * per_pair, axis=0) for kind in range(3)])
    places = jnp.stack([jnp.roll(find, kind * per_pair, axis=1) for kind in range(3)])
    message = (devices, stride, tokens)
    (sent,) = call(
        functools.partial(backward_kernel, per_pair),
        [(message, BF16)],
        [
            slope_all,
            hidden_all,
            gate_weight,
            up_weight,
            down_weight,
            kept,
            scale,
            child_gate,
            child_up,
            child_hid,
            select,
        ],
        limit=8,
        name="backward",
        scratch=[pltpu.VMEM(message, F32)],
    )
    received = lax.all_to_all(sent, "fsdp", 0, 0, tiled=True)
    anywhere = pl.BlockSpec(memory_space=pl.ANY)
    grad = ((parent_rows, features), BF16)
    *grads, gain_grad, loss_value = call(
        functools.partial(rows_kernel, per_pair),
        [grad, grad, grad, ((1, width), F32), ((1, 1), F32)],
        [received, places, hidden_all, scale, gains[1], slope_all],
        limit=16,
        name="rows",
        scratch=[
            pltpu.VMEM((3, parent_rows, features), BF16),
            pltpu.SemaphoreType.DMA((3, features // min(features, 1024))),
        ],
        specs=[anywhere] * 3 + [VMEM] * 2,
    )
    return (*grads, gain_grad.reshape(width), loss_value.reshape(1))


def solution(mesh):
    placed = (
        P("groups", "fsdp"),
        P("groups"),
        P("groups"),
        P(("groups", "fsdp"), None),
        P(("groups", "fsdp"), None),
        P(("groups", "fsdp"), None),
        P("groups"),
        P("groups"),
    )
    return jax.shard_map(
        shards,
        mesh=mesh,
        in_specs=placed,
        out_specs=(
            P(("groups", "fsdp"), None),
            P(("groups", "fsdp"), None),
            P(("groups", "fsdp"), None),
            P(("groups", "fsdp")),
            P("groups"),
        ),
        check_vma=False,
    )
```

```python
import functools

import jax
import jax.numpy as jnp
from jax import lax
from jax.experimental import pallas as pl
from jax.experimental.pallas import tpu as pltpu
from jax.sharding import PartitionSpec as P

BF16 = jnp.bfloat16
F32 = jnp.float32
NT = (((1,), (1,)), ((), ()))


def dot(left, right):
    return jnp.dot(left, right, preferred_element_type=F32)


def dot_nt(left, right):
    return lax.dot_general(left, right, NT, preferred_element_type=F32)


def after(value, other):
    return lax.optimization_barrier((value, other))[0]


def place(whole, part, owner):
    return lax.dynamic_update_slice(whole, part, (0, owner * part.shape[1]))


class Ring:
    def __init__(self, devices):
        self.devices = devices
        self.chips = devices // 2
        self.up_steps = self.chips // 2
        self.down_steps = self.chips - 1 - self.up_steps
        self.sibling = [(i, i ^ 1) for i in range(devices)]

    def owner(self, device, distance, core):
        return 2 * ((device // 2 + distance) % self.chips) + (device % 2 + core) % 2

    def shift(self, step):
        return [(i, (i + 2 * step) % self.devices) for i in range(self.devices)]

    def gather(self, block, device):
        tokens, width = block.shape
        whole = jnp.zeros((tokens, width * self.devices), block.dtype)

        def put(whole, part, distance):
            whole = place(whole, part, self.owner(device, distance, 0))
            other = lax.ppermute(part, "fsdp", self.sibling)
            return place(whole, other, self.owner(device, distance, 1))

        whole = put(whole, block, 0)
        up = down = block
        for step in range(1, self.up_steps + 1):
            up = lax.ppermute(up, "fsdp", self.shift(1))
            if step <= self.down_steps:
                down = lax.ppermute(down, "fsdp", self.shift(-1))
            whole = put(whole, up, self.chips - step)
            if step <= self.down_steps:
                whole = put(whole, down, step)
        return whole, block

    def scatter_sum(self, keep, other):
        swapped = lax.ppermute(other, "fsdp", self.sibling)

        def term(distance):
            return keep[distance] + swapped[distance]

        up = term(self.up_steps)
        down = term(self.up_steps + 1) if self.down_steps else None
        for step in range(1, self.up_steps + 1):
            up = lax.ppermute(up.astype(BF16), "fsdp", self.shift(1)).astype(F32)
            if step <= self.down_steps:
                down = lax.ppermute(down.astype(BF16), "fsdp", self.shift(-1)).astype(F32)
            if step < self.up_steps:
                up = up + term(self.up_steps - step)
            if step < self.down_steps:
                down = down + term(self.up_steps + 1 + step)
        total = term(0) + up
        return (total + down if self.down_steps else total), keep


class Grid(Ring):
    FAR_FIRST = (3, 2, 1, 0)

    def across(self, bits):
        return [(i, i ^ bits) for i in range(self.devices)]

    def owner(self, device, distance, core):
        return jnp.bitwise_xor(device, 2 * distance + core)

    def gather(self, block, device):
        tokens, width = block.shape
        whole = jnp.zeros((tokens, width * self.devices), block.dtype)
        column = {0: block}
        for z in (1, 2):
            column[z] = lax.ppermute(block, "fsdp", self.across(4 * z))
        column[3] = lax.ppermute(after(block, column[1]), "fsdp", self.across(12))
        for z in range(4):
            for y in range(2):
                part = lax.ppermute(column[z], "fsdp", self.across(2)) if y else column[z]
                whole = place(whole, part, self.owner(device, 2 * z + y, 0))
                part = lax.ppermute(part, "fsdp", self.sibling)
                whole = place(whole, part, self.owner(device, 2 * z + y, 1))
        return whole, column[1]

    def scatter_sum(self, keep, other):
        over_y = {}
        mine = {}
        sent = None
        for z in self.FAR_FIRST:
            pair = slice(2 * z, 2 * z + 2)
            part = lax.ppermute(other[pair], "fsdp", self.sibling)
            if sent is not None:
                part = after(part, sent)
            part = keep[pair] + part
            sent = part[1].astype(BF16)
            mine[z] = part[0]
            over_y[z] = lax.ppermute(sent, "fsdp", self.across(2))
        arrived = []
        sent = None
        for z in self.FAR_FIRST:
            part = over_y[z] if sent is None else after(over_y[z], sent)
            total = mine[z] + part.astype(F32)
            if z:
                sent = total.astype(BF16)
                arrived.append(lax.ppermute(sent, "fsdp", self.across(4 * z)))
        for part in arrived:
            total = total + part.astype(F32)
        return total, sent


def kept_rows(kept_index, device, parent_rows):
    local = kept_index[:, None] - device * parent_rows
    kept = jnp.any(local == jnp.arange(parent_rows)[None, :], axis=0)
    return kept.astype(F32).reshape(1, parent_rows)


def routing(kept_index, tile_owner, device, devices, parent_rows, stride):
    tile_count = tile_owner.shape[0]
    tile_rows = kept_index.shape[0] // tile_count
    slots = devices * stride
    layout = kept_index.reshape(tile_count, tile_rows)
    local = layout - device * parent_rows
    mine = (local >= 0) & (local < parent_rows)
    earlier = jnp.arange(tile_rows)[:, None] < jnp.arange(tile_rows)[None, :]
    position = dot(mine.astype(BF16), earlier.astype(BF16)).astype(jnp.int32)
    slot = jnp.where(mine, tile_owner[:, None] * stride + position, -1).reshape(-1)
    at_slot = (slot[None, :] == jnp.arange(slots)[:, None]).astype(BF16)
    at_row = (local.reshape(-1)[:, None] == jnp.arange(parent_rows)[None, :]).astype(BF16)
    send = dot(at_slot, at_row).astype(BF16)
    tile = jnp.sum(jnp.where((tile_owner == device)[:, None], layout, 0), axis=0)
    source = jnp.where(tile >= 0, tile // parent_rows, -1)
    same = (source[:, None] == source[None, :]) & earlier.T
    rank = jnp.sum(same.astype(jnp.int32), axis=1)
    slot = jnp.where(tile >= 0, source * stride + rank, -slots)
    find = (slot[:, None] == jnp.arange(slots)[None, :]).astype(BF16)
    return send, find


def forward_kernel(
    ring,
    hidden,
    parent_gain,
    child_gain,
    gate,
    up,
    down,
    kept,
    scale,
    child_gate,
    child_up,
    child_hid,
    keep,
    send,
):
    tokens, features = hidden.shape
    width = features // ring.devices
    pieces = 16
    piece = features // pieces
    cuts = [slice(k * piece, (k + 1) * piece) for k in range(pieces)]
    squares = jnp.zeros((tokens, piece), F32)
    for cols in cuts:
        h = hidden[:, cols].astype(F32)
        squares = squares + h * h
    mean = jnp.sum(squares, axis=1, keepdims=True) / features
    inverse = 1.0 / jnp.sqrt(mean + 1e-05)
    scale[...] = jnp.broadcast_to(inverse, scale.shape)
    gate_both = jnp.zeros((2 * tokens, gate.shape[0]), F32)
    up_both = jnp.zeros((2 * tokens, gate.shape[0]), F32)
    for cols in cuts:
        normed = hidden[:, cols].astype(F32) * inverse
        parent = (normed * parent_gain[:, cols]).astype(BF16)
        child = (normed * child_gain[:, cols]).astype(BF16)
        both = jnp.concatenate([parent, child], axis=0)
        gate_both = gate_both + dot_nt(both, gate[:, cols])
        up_both = up_both + dot_nt(both, up[:, cols])
    hid = gate_both * jax.nn.sigmoid(gate_both) * up_both
    child_gate[...] = gate_both[tokens:]
    child_up[...] = up_both[tokens:]
    child = jnp.where(kept[...] > 0, hid[tokens:], 0.0).astype(BF16)
    child_hid[...] = child
    both_hid = jnp.concatenate([child, -hid[:tokens].astype(BF16)], axis=0)
    device = lax.axis_index("fsdp")
    for core, target in ((1, send), (0, keep)):
        for distance in range(ring.chips):
            start = ring.owner(device, distance, core) * width
            out = dot(both_hid, down[:, pl.ds(pl.multiple_of(start, width), width)])
            target[distance] = out[:tokens] + out[tokens:]


def backward_kernel(
    per_pair,
    slope,
    hidden,
    gate,
    up,
    down,
    kept,
    scale,
    child_gate,
    child_up,
    child_hid,
    select,
    sent,
    message,
):
    devices, stride, _ = message.shape
    tokens = slope.shape[0]
    width = slope.shape[1] // devices
    child_slope = dot_nt(slope[...], down[...])
    g, u = child_gate[...], child_up[...]
    sig = jax.nn.sigmoid(g)
    live = kept[...] > 0
    gate_back = child_slope * u * sig * (1.0 + g * (1.0 - sig))
    gate_back = jnp.where(live, gate_back, 0.0).astype(BF16)
    up_back = jnp.where(live, child_slope * g * sig, 0.0).astype(BF16)
    rows = dot_nt(select[0], gate_back) + dot_nt(select[1], up_back)
    rows = rows + dot_nt(select[2], child_hid[...])
    message[...] = rows.reshape(devices, stride, tokens)
    inverse = scale[...][:, :1]
    high_at, gain_rows = 3 * per_pair, width // 128
    for k in range(devices):
        cols = slice(k * width, (k + 1) * width)
        input_slope = dot(gate_back, gate[:, cols]) + dot(up_back, up[:, cols])
        normed = hidden[:, cols].astype(F32) * inverse
        part = jnp.sum(input_slope * normed, axis=0, keepdims=True)
        high = part.astype(BF16).astype(F32)
        for r in range(gain_rows):
            lanes = slice(r * 128, (r + 1) * 128)
            at = high_at + r
            message[k, at : at + 1, :] = high[:, lanes]
            at = at + gain_rows
            message[k, at : at + 1, :] = (part - high)[:, lanes]
    sent[...] = message[...].astype(BF16)


def prepare_kernel(hidden, scale, child_gain, slope, child_in, loss):
    tokens, features = hidden.shape
    inverse = scale[...][:, :1]
    cut = min(features, 512)
    squares = jnp.zeros((tokens, cut), F32)
    for k in range(features // cut):
        cols = slice(k * cut, (k + 1) * cut)
        difference = slope[:, cols].astype(F32)
        squares = squares + difference * difference
        child = hidden[:, cols].astype(F32) * inverse * child_gain[:, cols]
        child_in[:, cols] = child.astype(BF16)
    squares = jnp.sum(jnp.sum(squares, axis=0, keepdims=True), axis=1, keepdims=True)
    loss[...] = 0.5 * squares / (tokens * features)


def rows_kernel(
    per_pair,
    received,
    places,
    child_in,
    slope,
    grad_gate,
    grad_up,
    grad_down,
    gain,
    made,
    done,
):
    rows, features = grad_gate.shape
    devices, stride, tokens = received.shape
    message = received[...].reshape(devices * stride, tokens)
    tiles = [dot(places[kind], message).astype(BF16) for kind in range(3)]
    both = jnp.concatenate(tiles[:2], axis=0)
    cut = min(features, 1024)
    copies = []
    for k in range(features // cut):
        cols = slice(k * cut, (k + 1) * cut)
        made[2, :, cols] = dot(tiles[2], slope[:, cols]).astype(BF16)
        out = dot(both, child_in[:, cols]).astype(BF16)
        made[0, :, cols] = out[:rows]
        made[1, :, cols] = out[rows:]
        for kind, grad in enumerate((grad_gate, grad_up, grad_down)):
            copy = pltpu.make_async_copy(made.at[kind, :, cols], grad.at[:, cols], done.at[kind, k])
            copy.start()
            copies.append(copy)
    total = jnp.sum(message.astype(F32).reshape(devices, stride, tokens), axis=0)
    gain_rows = gain.shape[1] // 128
    for r in range(gain_rows):
        at = 3 * per_pair + r
        gain[:, r * 128 : (r + 1) * 128] = (
            total[at : at + 1, :] + total[at + gain_rows : at + gain_rows + 1, :]
        )
    for copy in copies:
        copy.wait()


VMEM = pl.BlockSpec(memory_space=pltpu.VMEM)
MIB = 1024 * 1024


def call(kernel, outs, operands, limit, name, scratch=(), specs=None):
    return pl.pallas_call(
        kernel,
        out_shape=[jax.ShapeDtypeStruct(shape, dtype) for shape, dtype in outs],
        in_specs=[VMEM] * len(operands),
        out_specs=specs or [VMEM] * len(outs),
        scratch_shapes=list(scratch),
        compiler_params=pltpu.CompilerParams(vmem_limit_bytes=limit * MIB),
        name=name,
    )(*operands)


def shards(
    hidden, parent_gain, child_gain, gate_weight, up_weight, down_weight, kept_index, tile_owner
):
    devices = lax.axis_size("fsdp")
    device = lax.axis_index("fsdp")
    ring = Grid(devices) if devices == 16 else Ring(devices)
    chips = ring.chips
    parent_rows = gate_weight.shape[0]
    tokens, width = hidden.shape
    features = width * devices
    per_pair = kept_index.shape[0] // tile_owner.shape[0] // devices
    stride = -(-(3 * per_pair + 2 * (width // 128)) // 8) * 8
    square = ((tokens, parent_rows), F32)
    gains = [parent_gain.reshape(1, features), child_gain.reshape(1, features)]
    hidden_all, early = ring.gather(hidden, device)
    kept = kept_rows(after(kept_index, early), device, parent_rows)
    scale, child_gate, child_up, child_hid, keep, other = call(
        functools.partial(forward_kernel, ring),
        [
            ((tokens, 128), F32),
            square,
            square,
            ((tokens, parent_rows), BF16),
            ((chips, tokens, width), F32),
            ((chips, tokens, width), F32),
        ],
        [
            hidden_all,
            *gains,
            gate_weight,
            up_weight,
            down_weight,
            kept,
        ],
        limit=6,
        name="forward",
    )
    difference, last_sent = ring.scatter_sum(keep, other)
    slope_all, _ = ring.gather(difference.astype(BF16), device)

    kept_index, tile_owner, _ = lax.optimization_barrier((kept_index, tile_owner, last_sent))
    send, find = routing(kept_index, tile_owner, device, devices, parent_rows, stride)
    select = jnp.stack([jnp.roll(send, kind * per_pair, axis=0) for kind in range(3)])
    places = jnp.stack([jnp.roll(find, kind * per_pair, axis=1) for kind in range(3)])
    message = (devices, stride, tokens)
    (sent,) = call(
        functools.partial(backward_kernel, per_pair),
        [(message, BF16)],
        [
            slope_all,
            hidden_all,
            gate_weight,
            up_weight,
            down_weight,
            kept,
            scale,
            child_gate,
            child_up,
            child_hid,
            select,
        ],
        limit=6,
        name="backward",
        scratch=[pltpu.VMEM(message, F32)],
    )
    received = lax.all_to_all(sent, "fsdp", 0, 0, tiled=True)
    anywhere = pl.BlockSpec(memory_space=pl.ANY)
    grad = ((parent_rows, features), BF16)
    child_in, loss_value = call(
        prepare_kernel,
        [((tokens, features), BF16), ((1, 1), F32)],
        [after(hidden_all, sent), scale, gains[1], slope_all],
        limit=6,
        name="prepare",
    )
    *grads, gain_grad = call(
        functools.partial(rows_kernel, per_pair),
        [grad, grad, grad, ((1, width), F32)],
        [received, places, child_in, slope_all],
        limit=8,
        name="rows",
        scratch=[
            pltpu.VMEM((3, parent_rows, features), BF16),
            pltpu.SemaphoreType.DMA((3, features // min(features, 1024))),
        ],
        specs=[anywhere] * 3 + [VMEM],
    )
    return (*grads, gain_grad.reshape(width), loss_value.reshape(1))


def solution(mesh):
    placed = (
        P("groups", "fsdp"),
        P("groups"),
        P("groups"),
        P(("groups", "fsdp"), None),
        P(("groups", "fsdp"), None),
        P(("groups", "fsdp"), None),
        P("groups"),
        P("groups"),
    )
    return jax.shard_map(
        shards,
        mesh=mesh,
        in_specs=placed,
        out_specs=(
            P(("groups", "fsdp"), None),
            P(("groups", "fsdp"), None),
            P(("groups", "fsdp"), None),
            P(("groups", "fsdp")),
            P("groups"),
        ),
        check_vma=False,
    )
```

```python
import functools

import jax
import jax.numpy as jnp
from jax import lax
from jax.experimental import pallas as pl
from jax.experimental.pallas import tpu as pltpu
from jax.sharding import PartitionSpec as P

BF16 = jnp.bfloat16
F32 = jnp.float32
NT = (((1,), (1,)), ((), ()))


def dot(left, right):
    return jnp.dot(left, right, preferred_element_type=F32)


def dot_nt(left, right):
    return lax.dot_general(left, right, NT, preferred_element_type=F32)


def after(value, other):
    return lax.optimization_barrier((value, other))[0]


def place(whole, part, owner):
    return lax.dynamic_update_slice(whole, part, (0, owner * part.shape[1]))


class Ring:
    def __init__(self, devices):
        self.devices = devices
        self.chips = devices // 2
        self.up_steps = self.chips // 2
        self.down_steps = self.chips - 1 - self.up_steps
        self.sibling = [(i, i ^ 1) for i in range(devices)]

    def owner(self, device, distance, core):
        return 2 * ((device // 2 + distance) % self.chips) + (device % 2 + core) % 2

    def shift(self, step):
        return [(i, (i + 2 * step) % self.devices) for i in range(self.devices)]

    def gather(self, block, device):
        tokens, width = block.shape
        whole = jnp.zeros((tokens, width * self.devices), block.dtype)

        def put(whole, part, distance):
            whole = place(whole, part, self.owner(device, distance, 0))
            other = lax.ppermute(part, "fsdp", self.sibling)
            return place(whole, other, self.owner(device, distance, 1))

        whole = put(whole, block, 0)
        up = down = block
        for step in range(1, self.up_steps + 1):
            up = lax.ppermute(up, "fsdp", self.shift(1))
            if step <= self.down_steps:
                down = lax.ppermute(down, "fsdp", self.shift(-1))
            whole = put(whole, up, self.chips - step)
            if step <= self.down_steps:
                whole = put(whole, down, step)
        return whole, block

    def scatter_sum(self, product):
        keep = product([], list(range(self.chips)), None)

        def term(distance):
            return keep[distance]

        up = term(self.up_steps)
        down = term(self.up_steps + 1) if self.down_steps else None
        for step in range(1, self.up_steps + 1):
            up = lax.ppermute(up.astype(BF16), "fsdp", self.shift(1)).astype(F32)
            if step <= self.down_steps:
                down = lax.ppermute(down.astype(BF16), "fsdp", self.shift(-1)).astype(F32)
            if step < self.up_steps:
                up = up + term(self.up_steps - step)
            if step < self.down_steps:
                down = down + term(self.up_steps + 1 + step)
        total = term(0) + up
        return (total + down if self.down_steps else total), keep[0]


class Grid(Ring):
    FAR_FIRST = (3, 2, 1, 0)

    def across(self, bits):
        return [(i, i ^ bits) for i in range(self.devices)]

    def owner(self, device, distance, core):
        return jnp.bitwise_xor(device, 2 * distance + core)

    def gather(self, block, device):
        tokens, width = block.shape
        whole = jnp.zeros((tokens, width * self.devices), block.dtype)
        column = {0: block}
        for z in (1, 2):
            column[z] = lax.ppermute(block, "fsdp", self.across(4 * z))
        column[3] = lax.ppermute(after(block, column[1]), "fsdp", self.across(12))
        for z in range(4):
            for y in range(2):
                part = lax.ppermute(column[z], "fsdp", self.across(2)) if y else column[z]
                whole = place(whole, part, self.owner(device, 2 * z + y, 0))
                part = lax.ppermute(part, "fsdp", self.sibling)
                whole = place(whole, part, self.owner(device, 2 * z + y, 1))
        return whole, column[1]

    def scatter_sum(self, product):
        over_y = {}
        mine = {}
        sent = None
        for z in self.FAR_FIRST:
            sent, mine[z] = product([2 * z + 1], [2 * z], sent)
            over_y[z] = lax.ppermute(sent, "fsdp", self.across(2))
        arrived = []
        sent = None
        for z in self.FAR_FIRST:
            part = over_y[z] if sent is None else after(over_y[z], sent)
            total = mine[z] + part.astype(F32)
            if z:
                sent = total.astype(BF16)
                arrived.append(lax.ppermute(sent, "fsdp", self.across(4 * z)))
        for part in arrived:
            total = total + part.astype(F32)
        return total, sent


def kept_rows(kept_index, device, parent_rows):
    local = kept_index[:, None] - device * parent_rows
    kept = jnp.any(local == jnp.arange(parent_rows)[None, :], axis=0)
    return kept.astype(F32).reshape(1, parent_rows)


def routing(kept_index, tile_owner, device, devices, parent_rows, stride):
    tile_count = tile_owner.shape[0]
    tile_rows = kept_index.shape[0] // tile_count
    slots = devices * stride
    layout = kept_index.reshape(tile_count, tile_rows)
    local = layout - device * parent_rows
    mine = (local >= 0) & (local < parent_rows)
    earlier = jnp.arange(tile_rows)[:, None] < jnp.arange(tile_rows)[None, :]
    position = dot(mine.astype(BF16), earlier.astype(BF16)).astype(jnp.int32)
    slot = jnp.where(mine, tile_owner[:, None] * stride + position, -1).reshape(-1)
    at_slot = (slot[None, :] == jnp.arange(slots)[:, None]).astype(BF16)
    at_row = (local.reshape(-1)[:, None] == jnp.arange(parent_rows)[None, :]).astype(BF16)
    send = dot(at_slot, at_row).astype(BF16)
    tile = jnp.sum(jnp.where((tile_owner == device)[:, None], layout, 0), axis=0)
    source = jnp.where(tile >= 0, tile // parent_rows, -1)
    same = (source[:, None] == source[None, :]) & earlier.T
    rank = jnp.sum(same.astype(jnp.int32), axis=1)
    slot = jnp.where(tile >= 0, source * stride + rank, -slots)
    find = (slot[:, None] == jnp.arange(slots)[None, :]).astype(BF16)
    return send, find


def forward_kernel(
    hidden, parent_gain, child_gain, gate, up, kept, scale, child_gate, child_up, both_hid
):
    tokens, features = hidden.shape
    pieces = 16
    piece = features // pieces
    cuts = [slice(k * piece, (k + 1) * piece) for k in range(pieces)]
    squares = jnp.zeros((tokens, piece), F32)
    for cols in cuts:
        h = hidden[:, cols].astype(F32)
        squares = squares + h * h
    mean = jnp.sum(squares, axis=1, keepdims=True) / features
    inverse = 1.0 / jnp.sqrt(mean + 1e-05)
    scale[...] = jnp.broadcast_to(inverse, scale.shape)
    rows = gate.shape[0]
    products = jnp.zeros((2 * tokens, 2 * rows), F32)
    for cols in cuts:
        normed = hidden[:, cols].astype(F32) * inverse
        parent = (normed * parent_gain[:, cols]).astype(BF16)
        child = (normed * child_gain[:, cols]).astype(BF16)
        both = jnp.concatenate([parent, child], axis=0)
        weights = jnp.concatenate([gate[:, cols], up[:, cols]], axis=0)
        products = products + dot_nt(both, weights)
    gate_both, up_both = products[:, :rows], products[:, rows:]
    hid = gate_both * jax.nn.sigmoid(gate_both) * up_both
    child_gate[...] = gate_both[tokens:]
    child_up[...] = up_both[tokens:]
    child = jnp.where(kept[...] > 0, hid[tokens:], 0.0).astype(BF16)
    both_hid[:tokens, :] = child
    both_hid[tokens:, :] = -hid[:tokens].astype(BF16)


def difference_kernel(ring, distances, hid, other_hid, down, other_down, *parts):
    tokens = hid.shape[0] // 2
    width = down.shape[1] // ring.devices
    device = lax.axis_index("fsdp")
    left = jnp.concatenate([hid[...], other_hid[...]], axis=1)
    for distance, part in zip(distances, parts):
        start = ring.owner(device, distance, 0) * width
        cols = pl.ds(pl.multiple_of(start, width), width)
        right = jnp.concatenate([down[:, cols], other_down[:, cols]], axis=0)
        out = dot(left, right)
        part[...] = (out[:tokens] + out[tokens:]).astype(part.dtype)


def backward_kernel(
    per_pair,
    slope,
    hidden,
    gate,
    up,
    down,
    kept,
    scale,
    child_gate,
    child_up,
    both_hid,
    select,
    sent,
    message,
):
    devices, stride, _ = message.shape
    tokens = slope.shape[0]
    width = slope.shape[1] // devices
    child_slope = dot_nt(slope[...], down[...])
    g, u = child_gate[...], child_up[...]
    sig = jax.nn.sigmoid(g)
    live = kept[...] > 0
    gate_back = child_slope * u * sig * (1.0 + g * (1.0 - sig))
    gate_back = jnp.where(live, gate_back, 0.0).astype(BF16)
    up_back = jnp.where(live, child_slope * g * sig, 0.0).astype(BF16)
    rows = dot_nt(select[0], gate_back) + dot_nt(select[1], up_back)
    rows = rows + dot_nt(select[2], both_hid[:tokens, :])
    message[...] = rows.reshape(devices, stride, tokens)
    both_back = jnp.concatenate([gate_back, up_back], axis=1)
    inverse = scale[...][:, :1]
    high_at, gain_rows = 3 * per_pair, width // 128
    for k in range(devices):
        cols = slice(k * width, (k + 1) * width)
        weights = jnp.concatenate([gate[:, cols], up[:, cols]], axis=0)
        input_slope = dot(both_back, weights)
        normed = hidden[:, cols].astype(F32) * inverse
        part = jnp.sum(input_slope * normed, axis=0, keepdims=True)
        high = part.astype(BF16).astype(F32)
        for r in range(gain_rows):
            lanes = slice(r * 128, (r + 1) * 128)
            at = high_at + r
            message[k, at : at + 1, :] = high[:, lanes]
            at = at + gain_rows
            message[k, at : at + 1, :] = (part - high)[:, lanes]
    sent[...] = message[...].astype(BF16)


def prepare_kernel(hidden, scale, child_gain, slope, child_in, loss):
    tokens, features = hidden.shape
    inverse = scale[...][:, :1]
    cut = min(features, 512)
    squares = jnp.zeros((tokens, cut), F32)
    for k in range(features // cut):
        cols = slice(k * cut, (k + 1) * cut)
        difference = slope[:, cols].astype(F32)
        squares = squares + difference * difference
        child = hidden[:, cols].astype(F32) * inverse * child_gain[:, cols]
        child_in[:, cols] = child.astype(BF16)
    squares = jnp.sum(jnp.sum(squares, axis=0, keepdims=True), axis=1, keepdims=True)
    loss[...] = 0.5 * squares / (tokens * features)


def rows_kernel(
    per_pair,
    received,
    places,
    child_in,
    slope,
    grad_gate,
    grad_up,
    grad_down,
    gain,
    made,
    done,
):
    rows, features = grad_gate.shape
    devices, stride, tokens = received.shape
    message = received[...].reshape(devices * stride, tokens)
    tiles = [dot(places[kind], message).astype(BF16) for kind in range(3)]
    both = jnp.concatenate(tiles[:2], axis=0)
    cut = min(features, 1024)
    copies = []
    for k in range(features // cut):
        cols = slice(k * cut, (k + 1) * cut)
        made[2, :, cols] = dot(tiles[2], slope[:, cols]).astype(BF16)
        out = dot(both, child_in[:, cols]).astype(BF16)
        made[0, :, cols] = out[:rows]
        made[1, :, cols] = out[rows:]
        for kind, grad in enumerate((grad_gate, grad_up, grad_down)):
            copy = pltpu.make_async_copy(made.at[kind, :, cols], grad.at[:, cols], done.at[kind, k])
            copy.start()
            copies.append(copy)
    total = jnp.sum(message.astype(F32).reshape(devices, stride, tokens), axis=0)
    gain_rows = gain.shape[1] // 128
    for r in range(gain_rows):
        at = 3 * per_pair + r
        gain[:, r * 128 : (r + 1) * 128] = (
            total[at : at + 1, :] + total[at + gain_rows : at + gain_rows + 1, :]
        )
    for copy in copies:
        copy.wait()


VMEM = pl.BlockSpec(memory_space=pltpu.VMEM)
MIB = 1024 * 1024


def call(kernel, outs, operands, limit, name, scratch=(), specs=None):
    return pl.pallas_call(
        kernel,
        out_shape=[jax.ShapeDtypeStruct(shape, dtype) for shape, dtype in outs],
        in_specs=[VMEM] * len(operands),
        out_specs=specs or [VMEM] * len(outs),
        scratch_shapes=list(scratch),
        compiler_params=pltpu.CompilerParams(vmem_limit_bytes=limit * MIB),
        name=name,
    )(*operands)


def shards(
    hidden, parent_gain, child_gain, gate_weight, up_weight, down_weight, kept_index, tile_owner
):
    devices = lax.axis_size("fsdp")
    device = lax.axis_index("fsdp")
    ring = Grid(devices) if devices == 16 else Ring(devices)
    chips = ring.chips
    parent_rows = gate_weight.shape[0]
    tokens, width = hidden.shape
    features = width * devices
    per_pair = kept_index.shape[0] // tile_owner.shape[0] // devices
    stride = -(-(3 * per_pair + 2 * (width // 128)) // 8) * 8
    square = ((tokens, parent_rows), F32)
    gains = [parent_gain.reshape(1, features), child_gain.reshape(1, features)]
    hidden_all, early = ring.gather(hidden, device)
    kept = kept_rows(after(kept_index, early), device, parent_rows)
    scale, child_gate, child_up, both_hid = call(
        forward_kernel,
        [((tokens, 128), F32), square, square, ((2 * tokens, parent_rows), BF16)],
        [hidden_all, *gains, gate_weight, up_weight, kept],
        limit=6,
        name="forward",
    )
    other_down = lax.ppermute(down_weight, "fsdp", ring.sibling)
    other_hid = lax.ppermute(both_hid, "fsdp", ring.sibling)

    def product(rounded, exact, previous):
        block = (tokens, width)
        hid = both_hid if previous is None else after(both_hid, previous)
        return call(
            functools.partial(difference_kernel, ring, rounded + exact),
            [(block, BF16)] * len(rounded) + [(block, F32)] * len(exact),
            [hid, other_hid, down_weight, other_down],
            limit=6,
            name="difference",
        )

    difference, last_sent = ring.scatter_sum(product)
    slope_all, _ = ring.gather(difference.astype(BF16), device)

    kept_index, tile_owner, _ = lax.optimization_barrier((kept_index, tile_owner, last_sent))
    send, find = routing(kept_index, tile_owner, device, devices, parent_rows, stride)
    select = jnp.stack([jnp.roll(send, kind * per_pair, axis=0) for kind in range(3)])
    places = jnp.stack([jnp.roll(find, kind * per_pair, axis=1) for kind in range(3)])
    message = (devices, stride, tokens)
    (sent,) = call(
        functools.partial(backward_kernel, per_pair),
        [(message, BF16)],
        [
            slope_all,
            hidden_all,
            gate_weight,
            up_weight,
            down_weight,
            kept,
            scale,
            child_gate,
            child_up,
            both_hid,
            select,
        ],
        limit=6,
        name="backward",
        scratch=[pltpu.VMEM(message, F32)],
    )
    received = lax.all_to_all(sent, "fsdp", 0, 0, tiled=True)
    anywhere = pl.BlockSpec(memory_space=pl.ANY)
    grad = ((parent_rows, features), BF16)
    child_in, loss_value = call(
        prepare_kernel,
        [((tokens, features), BF16), ((1, 1), F32)],
        [after(hidden_all, sent), scale, gains[1], slope_all],
        limit=6,
        name="prepare",
    )
    *grads, gain_grad = call(
        functools.partial(rows_kernel, per_pair),
        [grad, grad, grad, ((1, width), F32)],
        [received, places, child_in, slope_all],
        limit=8,
        name="rows",
        scratch=[
            pltpu.VMEM((3, parent_rows, features), BF16),
            pltpu.SemaphoreType.DMA((3, features // min(features, 1024))),
        ],
        specs=[anywhere] * 3 + [VMEM],
    )
    return (*grads, gain_grad.reshape(width), loss_value.reshape(1))


def solution(mesh):
    placed = (
        P("groups", "fsdp"),
        P("groups"),
        P("groups"),
        P(("groups", "fsdp"), None),
        P(("groups", "fsdp"), None),
        P(("groups", "fsdp"), None),
        P("groups"),
        P("groups"),
    )
    return jax.shard_map(
        shards,
        mesh=mesh,
        in_specs=placed,
        out_specs=(
            P(("groups", "fsdp"), None),
            P(("groups", "fsdp"), None),
            P(("groups", "fsdp"), None),
            P(("groups", "fsdp")),
            P("groups"),
        ),
        check_vma=False,
    )
```

```python
import functools

import jax
import jax.numpy as jnp
from jax import lax
from jax.experimental import pallas as pl
from jax.experimental.pallas import tpu as pltpu
from jax.sharding import PartitionSpec as P

BF16 = jnp.bfloat16
F32 = jnp.float32
NT = (((1,), (1,)), ((), ()))


def dot(left, right):
    return jnp.dot(left, right, preferred_element_type=F32)


def dot_nt(left, right):
    return lax.dot_general(left, right, NT, preferred_element_type=F32)


def after(value, other):
    return lax.optimization_barrier((value, other))[0]


def place(whole, part, owner):
    return lax.dynamic_update_slice(whole, part, (0, owner * part.shape[1]))


class Ring:
    EARLY = 1

    def __init__(self, devices):
        self.devices = devices
        self.chips = devices // 2
        self.up_steps = self.chips // 2
        self.down_steps = self.chips - 1 - self.up_steps
        self.sibling = [(i, i ^ 1) for i in range(devices)]
        at = [(j, core) for j in range(self.chips) for core in (0, 1)]
        self.first_at, self.late_at = at[: self.EARLY], at[self.EARLY :]

    def owner(self, device, distance, core):
        return 2 * ((device // 2 + distance) % self.chips) + (device % 2 + core) % 2

    def shift(self, step):
        return [(i, (i + 2 * step) % self.devices) for i in range(self.devices)]

    def gather(self, block, device):
        tokens, width = block.shape
        whole = jnp.zeros((tokens, width * self.devices), block.dtype)

        def put(whole, part, distance):
            whole = place(whole, part, self.owner(device, distance, 0))
            other = lax.ppermute(part, "fsdp", self.sibling)
            return place(whole, other, self.owner(device, distance, 1))

        whole = put(whole, block, 0)
        up = down = block
        for step in range(1, self.up_steps + 1):
            up = lax.ppermute(up, "fsdp", self.shift(1))
            if step <= self.down_steps:
                down = lax.ppermute(down, "fsdp", self.shift(-1))
            whole = put(whole, up, self.chips - step)
            if step <= self.down_steps:
                whole = put(whole, down, step)
        return whole, [block], block

    def scatter_sum(self, product):
        keep = product([], list(range(self.chips)), None)

        def term(distance):
            return keep[distance]

        up = term(self.up_steps)
        down = term(self.up_steps + 1) if self.down_steps else None
        for step in range(1, self.up_steps + 1):
            up = lax.ppermute(up.astype(BF16), "fsdp", self.shift(1)).astype(F32)
            if step <= self.down_steps:
                down = lax.ppermute(down.astype(BF16), "fsdp", self.shift(-1)).astype(F32)
            if step < self.up_steps:
                up = up + term(self.up_steps - step)
            if step < self.down_steps:
                down = down + term(self.up_steps + 1 + step)
        total = term(0) + up
        return (total + down if self.down_steps else total), keep[0]


class Grid(Ring):
    FAR_FIRST = (3, 2, 1, 0)
    EARLY = 12

    def across(self, bits):
        return [(i, i ^ bits) for i in range(self.devices)]

    def owner(self, device, distance, core):
        return jnp.bitwise_xor(device, 2 * distance + core)

    def gather(self, block, device):
        first = []
        tokens, width = block.shape
        whole = jnp.zeros((tokens, width * self.devices), block.dtype)
        column = {0: block}
        for z in (1, 2):
            column[z] = lax.ppermute(block, "fsdp", self.across(4 * z))
        column[3] = lax.ppermute(after(block, column[1]), "fsdp", self.across(12))
        for z in range(4):
            for y in range(2):
                part = lax.ppermute(column[z], "fsdp", self.across(2)) if y else column[z]
                whole = place(whole, part, self.owner(device, 2 * z + y, 0))
                other = lax.ppermute(part, "fsdp", self.sibling)
                whole = place(whole, other, self.owner(device, 2 * z + y, 1))
                if z < 3:
                    first += [part, other]
        return whole, first, column[1]

    def scatter_sum(self, product):
        over_y = {}
        mine = {}
        sent = None
        for z in self.FAR_FIRST:
            sent, mine[z] = product([2 * z + 1], [2 * z], sent)
            over_y[z] = lax.ppermute(sent, "fsdp", self.across(2))
        arrived = []
        sent = None
        for z in self.FAR_FIRST:
            part = over_y[z] if sent is None else after(over_y[z], sent)
            total = mine[z] + part.astype(F32)
            if z:
                sent = total.astype(BF16)
                arrived.append(lax.ppermute(sent, "fsdp", self.across(4 * z)))
        for part in arrived:
            total = total + part.astype(F32)
        return total, sent


def kept_rows(kept_index, device, parent_rows):
    local = kept_index[:, None] - device * parent_rows
    kept = jnp.any(local == jnp.arange(parent_rows)[None, :], axis=0)
    return kept.astype(F32).reshape(1, parent_rows)


def routing(kept_index, tile_owner, device, devices, parent_rows, stride):
    tile_count = tile_owner.shape[0]
    tile_rows = kept_index.shape[0] // tile_count
    slots = devices * stride
    layout = kept_index.reshape(tile_count, tile_rows)
    local = layout - device * parent_rows
    mine = (local >= 0) & (local < parent_rows)
    earlier = jnp.arange(tile_rows)[:, None] < jnp.arange(tile_rows)[None, :]
    position = dot(mine.astype(BF16), earlier.astype(BF16)).astype(jnp.int32)
    slot = jnp.where(mine, tile_owner[:, None] * stride + position, -1).reshape(-1)
    at_slot = (slot[None, :] == jnp.arange(slots)[:, None]).astype(BF16)
    at_row = (local.reshape(-1)[:, None] == jnp.arange(parent_rows)[None, :]).astype(BF16)
    send = dot(at_slot, at_row).astype(BF16)
    tile = jnp.sum(jnp.where((tile_owner == device)[:, None], layout, 0), axis=0)
    source = jnp.where(tile >= 0, tile // parent_rows, -1)
    same = (source[:, None] == source[None, :]) & earlier.T
    rank = jnp.sum(same.astype(jnp.int32), axis=1)
    slot = jnp.where(tile >= 0, source * stride + rank, -slots)
    find = (slot[:, None] == jnp.arange(slots)[None, :]).astype(BF16)
    return send, find


def squares_kernel(*refs):
    blocks, squares = refs[:-1], refs[-1]
    total = jnp.zeros(blocks[0].shape, F32)
    for block in blocks:
        h = block[...].astype(F32)
        total = total + h * h
    squares[...] = jnp.broadcast_to(jnp.sum(total, axis=1, keepdims=True), squares.shape)


def forward_kernel(
    ring, early, hidden, parent_gain, child_gain, gate, up, kept, scale, child_gate, child_up, both_hid
):
    tokens, features = hidden.shape
    pieces = 16
    piece = features // pieces
    cuts = [slice(k * piece, (k + 1) * piece) for k in range(pieces)]
    width = features // ring.devices
    device = lax.axis_index("fsdp")
    squares = jnp.zeros((tokens, width), F32)
    for at in ring.late_at:
        start = ring.owner(device, *at) * width
        h = hidden[:, pl.ds(pl.multiple_of(start, width), width)].astype(F32)
        squares = squares + h * h
    mean = (early[...][:, :1] + jnp.sum(squares, axis=1, keepdims=True)) / features
    inverse = 1.0 / jnp.sqrt(mean + 1e-05)
    scale[...] = jnp.broadcast_to(inverse, scale.shape)
    rows = gate.shape[0]
    products = jnp.zeros((2 * tokens, 2 * rows), F32)
    for cols in cuts:
        normed = hidden[:, cols].astype(F32) * inverse
        parent = (normed * parent_gain[:, cols]).astype(BF16)
        child = (normed * child_gain[:, cols]).astype(BF16)
        both = jnp.concatenate([parent, child], axis=0)
        weights = jnp.concatenate([gate[:, cols], up[:, cols]], axis=0)
        products = products + dot_nt(both, weights)
    gate_both, up_both = products[:, :rows], products[:, rows:]
    hid = gate_both * jax.nn.sigmoid(gate_both) * up_both
    child_gate[...] = gate_both[tokens:]
    child_up[...] = up_both[tokens:]
    child = jnp.where(kept[...] > 0, hid[tokens:], 0.0).astype(BF16)
    both_hid[:tokens, :] = child
    both_hid[tokens:, :] = -hid[:tokens].astype(BF16)


def difference_kernel(ring, distances, hid, other_hid, down, other_down, *parts):
    tokens = hid.shape[0] // 2
    width = down.shape[1] // ring.devices
    device = lax.axis_index("fsdp")
    left = jnp.concatenate([hid[...], other_hid[...]], axis=1)
    for distance, part in zip(distances, parts):
        start = ring.owner(device, distance, 0) * width
        cols = pl.ds(pl.multiple_of(start, width), width)
        right = jnp.concatenate([down[:, cols], other_down[:, cols]], axis=0)
        out = dot(left, right)
        part[...] = (out[:tokens] + out[tokens:]).astype(part.dtype)


def early_kernel(ring, *refs):
    blocks, (down, partial) = refs[:-2], refs[-2:]
    tokens, width = blocks[0].shape
    device = lax.axis_index("fsdp")
    total = jnp.zeros(partial.shape, F32)
    for block, at in zip(blocks, ring.first_at):
        start = ring.owner(device, *at) * width
        cols = pl.ds(pl.multiple_of(start, width), width)
        total = total + dot_nt(block[...], down[:, cols])
    partial[...] = total


def backward_kernel(
    per_pair,
    ring,
    partial,
    slope,
    hidden,
    gate,
    up,
    down,
    kept,
    scale,
    child_gate,
    child_up,
    both_hid,
    select,
    sent,
    message,
):
    devices, stride, _ = message.shape
    tokens = slope.shape[0]
    width = slope.shape[1] // devices
    device = lax.axis_index("fsdp")
    child_slope = partial[...]
    for at in ring.late_at:
        start = ring.owner(device, *at) * width
        cols = pl.ds(pl.multiple_of(start, width), width)
        child_slope = child_slope + dot_nt(slope[:, cols], down[:, cols])
    g, u = child_gate[...], child_up[...]
    sig = jax.nn.sigmoid(g)
    live = kept[...] > 0
    gate_back = child_slope * u * sig * (1.0 + g * (1.0 - sig))
    gate_back = jnp.where(live, gate_back, 0.0).astype(BF16)
    up_back = jnp.where(live, child_slope * g * sig, 0.0).astype(BF16)
    rows = dot_nt(select[0], gate_back) + dot_nt(select[1], up_back)
    rows = rows + dot_nt(select[2], both_hid[:tokens, :])
    message[...] = rows.reshape(devices, stride, tokens)
    both_back = jnp.concatenate([gate_back, up_back], axis=1)
    inverse = scale[...][:, :1]
    high_at, gain_rows = 3 * per_pair, width // 128
    for k in range(devices):
        cols = slice(k * width, (k + 1) * width)
        weights = jnp.concatenate([gate[:, cols], up[:, cols]], axis=0)
        input_slope = dot(both_back, weights)
        normed = hidden[:, cols].astype(F32) * inverse
        part = jnp.sum(input_slope * normed, axis=0, keepdims=True)
        high = part.astype(BF16).astype(F32)
        for r in range(gain_rows):
            lanes = slice(r * 128, (r + 1) * 128)
            at = high_at + r
            message[k, at : at + 1, :] = high[:, lanes]
            at = at + gain_rows
            message[k, at : at + 1, :] = (part - high)[:, lanes]
    sent[...] = message[...].astype(BF16)


def prepare_kernel(hidden, scale, child_gain, slope, child_in, loss):
    tokens, features = hidden.shape
    inverse = scale[...][:, :1]
    cut = min(features, 512)
    squares = jnp.zeros((tokens, cut), F32)
    for k in range(features // cut):
        cols = slice(k * cut, (k + 1) * cut)
        difference = slope[:, cols].astype(F32)
        squares = squares + difference * difference
        child = hidden[:, cols].astype(F32) * inverse * child_gain[:, cols]
        child_in[:, cols] = child.astype(BF16)
    squares = jnp.sum(jnp.sum(squares, axis=0, keepdims=True), axis=1, keepdims=True)
    loss[...] = 0.5 * squares / (tokens * features)


def rows_kernel(
    per_pair,
    received,
    places,
    child_in,
    slope,
    grad_gate,
    grad_up,
    grad_down,
    gain,
    made,
    done,
):
    rows, features = grad_gate.shape
    devices, stride, tokens = received.shape
    message = received[...].reshape(devices * stride, tokens)
    tiles = [dot(places[kind], message).astype(BF16) for kind in range(3)]
    empty = jnp.zeros_like(tiles[0])
    left = jnp.concatenate(
        [
            jnp.concatenate([tiles[0], empty], axis=1),
            jnp.concatenate([tiles[1], empty], axis=1),
            jnp.concatenate([empty, tiles[2]], axis=1),
        ],
        axis=0,
    )
    cut = min(features, 1024)
    copies = []
    for k in range(features // cut):
        cols = slice(k * cut, (k + 1) * cut)
        right = jnp.concatenate([child_in[:, cols], slope[:, cols]], axis=0)
        out = dot(left, right).astype(BF16)
        for kind in range(3):
            made[kind, :, cols] = out[kind * rows : (kind + 1) * rows]
        for kind, grad in enumerate((grad_gate, grad_up, grad_down)):
            copy = pltpu.make_async_copy(made.at[kind, :, cols], grad.at[:, cols], done.at[kind, k])
            copy.start()
            copies.append(copy)
    total = jnp.sum(message.astype(F32).reshape(devices, stride, tokens), axis=0)
    gain_rows = gain.shape[1] // 128
    for r in range(gain_rows):
        at = 3 * per_pair + r
        gain[:, r * 128 : (r + 1) * 128] = (
            total[at : at + 1, :] + total[at + gain_rows : at + gain_rows + 1, :]
        )
    for copy in copies:
        copy.wait()


VMEM = pl.BlockSpec(memory_space=pltpu.VMEM)
MIB = 1024 * 1024


def call(kernel, outs, operands, limit, name, scratch=(), specs=None):
    return pl.pallas_call(
        kernel,
        out_shape=[jax.ShapeDtypeStruct(shape, dtype) for shape, dtype in outs],
        in_specs=[VMEM] * len(operands),
        out_specs=specs or [VMEM] * len(outs),
        scratch_shapes=list(scratch),
        compiler_params=pltpu.CompilerParams(vmem_limit_bytes=limit * MIB),
        name=name,
    )(*operands)


def shards(
    hidden, parent_gain, child_gain, gate_weight, up_weight, down_weight, kept_index, tile_owner
):
    devices = lax.axis_size("fsdp")
    device = lax.axis_index("fsdp")
    ring = Grid(devices) if devices == 16 else Ring(devices)
    chips = ring.chips
    parent_rows = gate_weight.shape[0]
    tokens, width = hidden.shape
    features = width * devices
    per_pair = kept_index.shape[0] // tile_owner.shape[0] // devices
    stride = -(-(3 * per_pair + 2 * (width // 128)) // 8) * 8
    square = ((tokens, parent_rows), F32)
    gains = [parent_gain.reshape(1, features), child_gain.reshape(1, features)]
    hidden_all, first, early = ring.gather(hidden, device)
    kept = kept_rows(after(kept_index, early), device, parent_rows)
    (early_squares,) = call(
        squares_kernel, [((tokens, 128), F32)], first, limit=6, name="squares"
    )
    scale, child_gate, child_up, both_hid = call(
        functools.partial(forward_kernel, ring),
        [((tokens, 128), F32), square, square, ((2 * tokens, parent_rows), BF16)],
        [early_squares, hidden_all, *gains, gate_weight, up_weight, kept],
        limit=6,
        name="forward",
    )
    other_down = lax.ppermute(down_weight, "fsdp", ring.sibling)
    other_hid = lax.ppermute(both_hid, "fsdp", ring.sibling)

    def product(rounded, exact, previous):
        block = (tokens, width)
        hid = both_hid if previous is None else after(both_hid, previous)
        return call(
            functools.partial(difference_kernel, ring, rounded + exact),
            [(block, BF16)] * len(rounded) + [(block, F32)] * len(exact),
            [hid, other_hid, down_weight, other_down],
            limit=6,
            name="difference",
        )

    difference, last_sent = ring.scatter_sum(product)
    slope_all, first_slope, _ = ring.gather(difference.astype(BF16), device)

    kept_index, tile_owner, _ = lax.optimization_barrier((kept_index, tile_owner, last_sent))
    send, find = routing(kept_index, tile_owner, device, devices, parent_rows, stride)
    select = jnp.stack([jnp.roll(send, kind * per_pair, axis=0) for kind in range(3)])
    places = jnp.stack([jnp.roll(find, kind * per_pair, axis=1) for kind in range(3)])
    message = (devices, stride, tokens)
    (partial,) = call(
        functools.partial(early_kernel, ring),
        [square],
        [*first_slope, down_weight],
        limit=6,
        name="early",
    )
    (sent,) = call(
        functools.partial(backward_kernel, per_pair, ring),
        [(message, BF16)],
        [
            partial,
            slope_all,
            hidden_all,
            gate_weight,
            up_weight,
            down_weight,
            kept,
            scale,
            child_gate,
            child_up,
            both_hid,
            select,
        ],
        limit=6,
        name="backward",
        scratch=[pltpu.VMEM(message, F32)],
    )
    received = lax.all_to_all(sent, "fsdp", 0, 0, tiled=True)
    anywhere = pl.BlockSpec(memory_space=pl.ANY)
    grad = ((parent_rows, features), BF16)
    child_in, loss_value = call(
        prepare_kernel,
        [((tokens, features), BF16), ((1, 1), F32)],
        [after(hidden_all, sent), scale, gains[1], slope_all],
        limit=6,
        name="prepare",
    )
    *grads, gain_grad = call(
        functools.partial(rows_kernel, per_pair),
        [grad, grad, grad, ((1, width), F32)],
        [received, places, child_in, slope_all],
        limit=8,
        name="rows",
        scratch=[
            pltpu.VMEM((3, parent_rows, features), BF16),
            pltpu.SemaphoreType.DMA((3, features // min(features, 1024))),
        ],
        specs=[anywhere] * 3 + [VMEM],
    )
    return (*grads, gain_grad.reshape(width), loss_value.reshape(1))


def solution(mesh):
    placed = (
        P("groups", "fsdp"),
        P("groups"),
        P("groups"),
        P(("groups", "fsdp"), None),
        P(("groups", "fsdp"), None),
        P(("groups", "fsdp"), None),
        P("groups"),
        P("groups"),
    )
    return jax.shard_map(
        shards,
        mesh=mesh,
        in_specs=placed,
        out_specs=(
            P(("groups", "fsdp"), None),
            P(("groups", "fsdp"), None),
            P(("groups", "fsdp"), None),
            P(("groups", "fsdp")),
            P("groups"),
        ),
        check_vma=False,
    )
```

```python
import functools

import jax
import jax.numpy as jnp
from jax import lax
from jax.experimental import pallas as pl
from jax.experimental.pallas import tpu as pltpu
from jax.sharding import PartitionSpec as P

BF16 = jnp.bfloat16
F32 = jnp.float32
NT = (((1,), (1,)), ((), ()))


def dot(left, right):
    return jnp.dot(left, right, preferred_element_type=F32)


def dot_nt(left, right):
    return lax.dot_general(left, right, NT, preferred_element_type=F32)


def after(value, other):
    return lax.optimization_barrier((value, other))[0]


def place(whole, part, owner):
    return lax.dynamic_update_slice(whole, part, (0, owner * part.shape[1]))


class Ring:
    EARLY = 1

    def __init__(self, devices):
        self.devices = devices
        self.chips = devices // 2
        self.up_steps = self.chips // 2
        self.down_steps = self.chips - 1 - self.up_steps
        self.sibling = [(i, i ^ 1) for i in range(devices)]
        at = [(j, core) for j in range(self.chips) for core in (0, 1)]
        self.first_at, self.late_at = at[: self.EARLY], at[self.EARLY :]

    def owner(self, device, distance, core):
        return 2 * ((device // 2 + distance) % self.chips) + (device % 2 + core) % 2

    def shift(self, step):
        return [(i, (i + 2 * step) % self.devices) for i in range(self.devices)]

    def gather(self, block, device):
        tokens, width = block.shape
        whole = jnp.zeros((tokens, width * self.devices), block.dtype)

        def put(whole, part, distance):
            whole = place(whole, part, self.owner(device, distance, 0))
            other = lax.ppermute(part, "fsdp", self.sibling)
            return place(whole, other, self.owner(device, distance, 1))

        whole = put(whole, block, 0)
        up = down = block
        for step in range(1, self.up_steps + 1):
            up = lax.ppermute(up, "fsdp", self.shift(1))
            if step <= self.down_steps:
                down = lax.ppermute(down, "fsdp", self.shift(-1))
            whole = put(whole, up, self.chips - step)
            if step <= self.down_steps:
                whole = put(whole, down, step)
        return whole, [block], block

    def scatter_sum(self, product):
        keep = product([], list(range(self.chips)), None)

        def term(distance):
            return keep[distance]

        up = term(self.up_steps)
        down = term(self.up_steps + 1) if self.down_steps else None
        for step in range(1, self.up_steps + 1):
            up = lax.ppermute(up.astype(BF16), "fsdp", self.shift(1)).astype(F32)
            if step <= self.down_steps:
                down = lax.ppermute(down.astype(BF16), "fsdp", self.shift(-1)).astype(F32)
            if step < self.up_steps:
                up = up + term(self.up_steps - step)
            if step < self.down_steps:
                down = down + term(self.up_steps + 1 + step)
        total = term(0) + up
        return (total + down if self.down_steps else total), keep[0]


class Grid(Ring):
    FAR_FIRST = (3, 2, 1, 0)
    EARLY = 14

    def across(self, bits):
        return [(i, i ^ bits) for i in range(self.devices)]

    def owner(self, device, distance, core):
        return jnp.bitwise_xor(device, 2 * distance + core)

    def gather(self, block, device):
        first = []
        tokens, width = block.shape
        whole = jnp.zeros((tokens, width * self.devices), block.dtype)
        column = {0: block}
        for z in (1, 2):
            column[z] = lax.ppermute(block, "fsdp", self.across(4 * z))
        column[3] = lax.ppermute(after(block, column[1]), "fsdp", self.across(12))
        for z in range(4):
            for y in range(2):
                part = lax.ppermute(column[z], "fsdp", self.across(2)) if y else column[z]
                whole = place(whole, part, self.owner(device, 2 * z + y, 0))
                other = lax.ppermute(part, "fsdp", self.sibling)
                whole = place(whole, other, self.owner(device, 2 * z + y, 1))
                if 2 * z + y < 7:
                    first += [part, other]
        return whole, first, column[1]

    def scatter_sum(self, product):
        over_y = {}
        mine = {}
        sent = None
        for z in self.FAR_FIRST:
            sent, mine[z] = product([2 * z + 1], [2 * z], sent)
            over_y[z] = lax.ppermute(sent, "fsdp", self.across(2))
        arrived = []
        sent = None
        for z in self.FAR_FIRST:
            part = over_y[z] if sent is None else after(over_y[z], sent)
            total = mine[z] + part.astype(F32)
            if z:
                sent = total.astype(BF16)
                arrived.append(lax.ppermute(sent, "fsdp", self.across(4 * z)))
        for part in arrived:
            total = total + part.astype(F32)
        return total, sent


def kept_rows(kept_index, device, parent_rows):
    local = kept_index[:, None] - device * parent_rows
    kept = jnp.any(local == jnp.arange(parent_rows)[None, :], axis=0)
    return kept.astype(F32).reshape(1, parent_rows)


def routing(kept_index, tile_owner, device, devices, parent_rows, stride):
    tile_count = tile_owner.shape[0]
    tile_rows = kept_index.shape[0] // tile_count
    slots = devices * stride
    layout = kept_index.reshape(tile_count, tile_rows)
    local = layout - device * parent_rows
    mine = (local >= 0) & (local < parent_rows)
    earlier = jnp.arange(tile_rows)[:, None] < jnp.arange(tile_rows)[None, :]
    position = dot(mine.astype(BF16), earlier.astype(BF16)).astype(jnp.int32)
    slot = jnp.where(mine, tile_owner[:, None] * stride + position, -1).reshape(-1)
    at_slot = (slot[None, :] == jnp.arange(slots)[:, None]).astype(BF16)
    at_row = (local.reshape(-1)[:, None] == jnp.arange(parent_rows)[None, :]).astype(BF16)
    send = dot(at_slot, at_row).astype(BF16)
    tile = jnp.sum(jnp.where((tile_owner == device)[:, None], layout, 0), axis=0)
    source = jnp.where(tile >= 0, tile // parent_rows, -1)
    same = (source[:, None] == source[None, :]) & earlier.T
    rank = jnp.sum(same.astype(jnp.int32), axis=1)
    slot = jnp.where(tile >= 0, source * stride + rank, -slots)
    find = (slot[:, None] == jnp.arange(slots)[None, :]).astype(BF16)
    return send, find


def squares_kernel(*refs):
    blocks, squares = refs[:-1], refs[-1]
    total = jnp.zeros(blocks[0].shape, F32)
    for block in blocks:
        h = block[...].astype(F32)
        total = total + h * h
    squares[...] = jnp.broadcast_to(jnp.sum(total, axis=1, keepdims=True), squares.shape)


def forward_kernel(
    ring, early, hidden, parent_gain, child_gain, gate, up, kept, scale, child_gate, child_up, both_hid
):
    tokens, features = hidden.shape
    pieces = 16
    piece = features // pieces
    cuts = [slice(k * piece, (k + 1) * piece) for k in range(pieces)]
    width = features // ring.devices
    device = lax.axis_index("fsdp")
    squares = jnp.zeros((tokens, width), F32)
    for at in ring.late_at:
        start = ring.owner(device, *at) * width
        h = hidden[:, pl.ds(pl.multiple_of(start, width), width)].astype(F32)
        squares = squares + h * h
    mean = (early[...][:, :1] + jnp.sum(squares, axis=1, keepdims=True)) / features
    inverse = 1.0 / jnp.sqrt(mean + 1e-05)
    scale[...] = jnp.broadcast_to(inverse, scale.shape)
    rows = gate.shape[0]
    products = jnp.zeros((2 * tokens, 2 * rows), F32)
    for cols in cuts:
        normed = hidden[:, cols].astype(F32) * inverse
        parent = (normed * parent_gain[:, cols]).astype(BF16)
        child = (normed * child_gain[:, cols]).astype(BF16)
        both = jnp.concatenate([parent, child], axis=0)
        weights = jnp.concatenate([gate[:, cols], up[:, cols]], axis=0)
        products = products + dot_nt(both, weights)
    gate_both, up_both = products[:, :rows], products[:, rows:]
    hid = gate_both * jax.nn.sigmoid(gate_both) * up_both
    child_gate[...] = gate_both[tokens:]
    child_up[...] = up_both[tokens:]
    child = jnp.where(kept[...] > 0, hid[tokens:], 0.0).astype(BF16)
    both_hid[:tokens, :] = child
    both_hid[tokens:, :] = -hid[:tokens].astype(BF16)


def difference_kernel(ring, distances, hid, other_hid, down, other_down, *parts):
    tokens = hid.shape[0] // 2
    width = down.shape[1] // ring.devices
    device = lax.axis_index("fsdp")
    left = jnp.concatenate([hid[...], other_hid[...]], axis=1)
    for distance, part in zip(distances, parts):
        start = ring.owner(device, distance, 0) * width
        cols = pl.ds(pl.multiple_of(start, width), width)
        right = jnp.concatenate([down[:, cols], other_down[:, cols]], axis=0)
        out = dot(left, right)
        part[...] = (out[:tokens] + out[tokens:]).astype(part.dtype)


def early_kernel(ring, *refs):
    blocks, (down, partial) = refs[:-2], refs[-2:]
    tokens, width = blocks[0].shape
    device = lax.axis_index("fsdp")
    total = jnp.zeros(partial.shape, F32)
    for block, at in zip(blocks, ring.first_at):
        start = ring.owner(device, *at) * width
        cols = pl.ds(pl.multiple_of(start, width), width)
        total = total + dot_nt(block[...], down[:, cols])
    partial[...] = total


def backward_kernel(
    per_pair,
    ring,
    partial,
    slope,
    hidden,
    gate,
    up,
    down,
    kept,
    scale,
    child_gate,
    child_up,
    both_hid,
    select,
    sent,
    message,
):
    devices, stride, _ = message.shape
    tokens = slope.shape[0]
    width = slope.shape[1] // devices
    device = lax.axis_index("fsdp")
    child_slope = partial[...]
    for at in ring.late_at:
        start = ring.owner(device, *at) * width
        cols = pl.ds(pl.multiple_of(start, width), width)
        child_slope = child_slope + dot_nt(slope[:, cols], down[:, cols])
    g, u = child_gate[...], child_up[...]
    sig = jax.nn.sigmoid(g)
    live = kept[...] > 0
    gate_back = child_slope * u * sig * (1.0 + g * (1.0 - sig))
    gate_back = jnp.where(live, gate_back, 0.0).astype(BF16)
    up_back = jnp.where(live, child_slope * g * sig, 0.0).astype(BF16)
    rows = dot_nt(select[0], gate_back) + dot_nt(select[1], up_back)
    rows = rows + dot_nt(select[2], both_hid[:tokens, :])
    message[...] = rows.reshape(devices, stride, tokens)
    both_back = jnp.concatenate([gate_back, up_back], axis=1)
    inverse = scale[...][:, :1]
    high_at, gain_rows = 3 * per_pair, width // 128
    for k in range(devices):
        cols = slice(k * width, (k + 1) * width)
        weights = jnp.concatenate([gate[:, cols], up[:, cols]], axis=0)
        input_slope = dot(both_back, weights)
        normed = hidden[:, cols].astype(F32) * inverse
        part = jnp.sum(input_slope * normed, axis=0, keepdims=True)
        high = part.astype(BF16).astype(F32)
        for r in range(gain_rows):
            lanes = slice(r * 128, (r + 1) * 128)
            at = high_at + r
            message[k, at : at + 1, :] = high[:, lanes]
            at = at + gain_rows
            message[k, at : at + 1, :] = (part - high)[:, lanes]
    sent[...] = message[...].astype(BF16)


def prepare_kernel(hidden, scale, child_gain, slope, child_in, loss):
    tokens, features = hidden.shape
    inverse = scale[...][:, :1]
    cut = min(features, 512)
    squares = jnp.zeros((tokens, cut), F32)
    for k in range(features // cut):
        cols = slice(k * cut, (k + 1) * cut)
        difference = slope[:, cols].astype(F32)
        squares = squares + difference * difference
        child = hidden[:, cols].astype(F32) * inverse * child_gain[:, cols]
        child_in[:, cols] = child.astype(BF16)
    squares = jnp.sum(jnp.sum(squares, axis=0, keepdims=True), axis=1, keepdims=True)
    loss[...] = 0.5 * squares / (tokens * features)


def rows_kernel(
    per_pair,
    received,
    places,
    child_in,
    slope,
    grad_gate,
    grad_up,
    grad_down,
    gain,
    made,
    done,
):
    rows, features = grad_gate.shape
    devices, stride, tokens = received.shape
    message = received[...].reshape(devices * stride, tokens)
    tiles = [dot(places[kind], message).astype(BF16) for kind in range(3)]
    empty = jnp.zeros_like(tiles[0])
    left = jnp.concatenate(
        [
            jnp.concatenate([tiles[0], empty], axis=1),
            jnp.concatenate([tiles[1], empty], axis=1),
            jnp.concatenate([empty, tiles[2]], axis=1),
        ],
        axis=0,
    )
    cut = min(features, 1024)
    copies = []
    for k in range(features // cut):
        cols = slice(k * cut, (k + 1) * cut)
        right = jnp.concatenate([child_in[:, cols], slope[:, cols]], axis=0)
        out = dot(left, right).astype(BF16)
        for kind in range(3):
            made[kind, :, cols] = out[kind * rows : (kind + 1) * rows]
        for kind, grad in enumerate((grad_gate, grad_up, grad_down)):
            copy = pltpu.make_async_copy(made.at[kind, :, cols], grad.at[:, cols], done.at[kind, k])
            copy.start()
            copies.append(copy)
    total = jnp.sum(message.astype(F32).reshape(devices, stride, tokens), axis=0)
    gain_rows = gain.shape[1] // 128
    for r in range(gain_rows):
        at = 3 * per_pair + r
        gain[:, r * 128 : (r + 1) * 128] = (
            total[at : at + 1, :] + total[at + gain_rows : at + gain_rows + 1, :]
        )
    for copy in copies:
        copy.wait()


VMEM = pl.BlockSpec(memory_space=pltpu.VMEM)
MIB = 1024 * 1024


def call(kernel, outs, operands, limit, name, scratch=(), specs=None):
    return pl.pallas_call(
        kernel,
        out_shape=[jax.ShapeDtypeStruct(shape, dtype) for shape, dtype in outs],
        in_specs=[VMEM] * len(operands),
        out_specs=specs or [VMEM] * len(outs),
        scratch_shapes=list(scratch),
        compiler_params=pltpu.CompilerParams(vmem_limit_bytes=limit * MIB),
        name=name,
    )(*operands)


def shards(
    hidden, parent_gain, child_gain, gate_weight, up_weight, down_weight, kept_index, tile_owner
):
    devices = lax.axis_size("fsdp")
    device = lax.axis_index("fsdp")
    ring = Grid(devices) if devices == 16 else Ring(devices)
    chips = ring.chips
    parent_rows = gate_weight.shape[0]
    tokens, width = hidden.shape
    features = width * devices
    per_pair = kept_index.shape[0] // tile_owner.shape[0] // devices
    stride = -(-(3 * per_pair + 2 * (width // 128)) // 8) * 8
    square = ((tokens, parent_rows), F32)
    gains = [parent_gain.reshape(1, features), child_gain.reshape(1, features)]
    hidden_all, first, early = ring.gather(hidden, device)
    kept = kept_rows(after(kept_index, early), device, parent_rows)
    (early_squares,) = call(
        squares_kernel, [((tokens, 128), F32)], first, limit=6, name="squares"
    )
    scale, child_gate, child_up, both_hid = call(
        functools.partial(forward_kernel, ring),
        [((tokens, 128), F32), square, square, ((2 * tokens, parent_rows), BF16)],
        [early_squares, hidden_all, *gains, gate_weight, up_weight, kept],
        limit=6,
        name="forward",
    )
    other_down = lax.ppermute(down_weight, "fsdp", ring.sibling)
    other_hid = lax.ppermute(both_hid, "fsdp", ring.sibling)

    def product(rounded, exact, previous):
        block = (tokens, width)
        hid = both_hid if previous is None else after(both_hid, previous)
        return call(
            functools.partial(difference_kernel, ring, rounded + exact),
            [(block, BF16)] * len(rounded) + [(block, F32)] * len(exact),
            [hid, other_hid, down_weight, other_down],
            limit=6,
            name="difference",
        )

    difference, last_sent = ring.scatter_sum(product)
    slope_all, first_slope, _ = ring.gather(difference.astype(BF16), device)

    kept_index, tile_owner, _ = lax.optimization_barrier((kept_index, tile_owner, last_sent))
    send, find = routing(kept_index, tile_owner, device, devices, parent_rows, stride)
    select = jnp.stack([jnp.roll(send, kind * per_pair, axis=0) for kind in range(3)])
    places = jnp.stack([jnp.roll(find, kind * per_pair, axis=1) for kind in range(3)])
    message = (devices, stride, tokens)
    (partial,) = call(
        functools.partial(early_kernel, ring),
        [square],
        [*first_slope, down_weight],
        limit=6,
        name="early",
    )
    (sent,) = call(
        functools.partial(backward_kernel, per_pair, ring),
        [(message, BF16)],
        [
            partial,
            slope_all,
            hidden_all,
            gate_weight,
            up_weight,
            down_weight,
            kept,
            scale,
            child_gate,
            child_up,
            both_hid,
            select,
        ],
        limit=6,
        name="backward",
        scratch=[pltpu.VMEM(message, F32)],
    )
    received = lax.all_to_all(sent, "fsdp", 0, 0, tiled=True)
    anywhere = pl.BlockSpec(memory_space=pl.ANY)
    grad = ((parent_rows, features), BF16)
    child_in, loss_value = call(
        prepare_kernel,
        [((tokens, features), BF16), ((1, 1), F32)],
        [after(hidden_all, sent), scale, gains[1], slope_all],
        limit=6,
        name="prepare",
    )
    *grads, gain_grad = call(
        functools.partial(rows_kernel, per_pair),
        [grad, grad, grad, ((1, width), F32)],
        [received, places, child_in, slope_all],
        limit=8,
        name="rows",
        scratch=[
            pltpu.VMEM((3, parent_rows, features), BF16),
            pltpu.SemaphoreType.DMA((3, features // min(features, 1024))),
        ],
        specs=[anywhere] * 3 + [VMEM],
    )
    return (*grads, gain_grad.reshape(width), loss_value.reshape(1))


def solution(mesh):
    placed = (
        P("groups", "fsdp"),
        P("groups"),
        P("groups"),
        P(("groups", "fsdp"), None),
        P(("groups", "fsdp"), None),
        P(("groups", "fsdp"), None),
        P("groups"),
        P("groups"),
    )
    return jax.shard_map(
        shards,
        mesh=mesh,
        in_specs=placed,
        out_specs=(
            P(("groups", "fsdp"), None),
            P(("groups", "fsdp"), None),
            P(("groups", "fsdp"), None),
            P(("groups", "fsdp")),
            P("groups"),
        ),
        check_vma=False,
    )
```

```python
import functools

import jax
import jax.numpy as jnp
from jax import lax
from jax.experimental import pallas as pl
from jax.experimental.pallas import tpu as pltpu
from jax.sharding import PartitionSpec as P

BF16 = jnp.bfloat16
F32 = jnp.float32
NT = (((1,), (1,)), ((), ()))


def dot(left, right):
    return jnp.dot(left, right, preferred_element_type=F32)


def dot_nt(left, right):
    return lax.dot_general(left, right, NT, preferred_element_type=F32)


def after(value, other):
    return lax.optimization_barrier((value, other))[0]


def place(whole, part, owner):
    return lax.dynamic_update_slice(whole, part, (0, owner * part.shape[1]))


class Ring:
    EARLY = 1

    def __init__(self, devices):
        self.devices = devices
        self.chips = devices // 2
        self.up_steps = self.chips // 2
        self.down_steps = self.chips - 1 - self.up_steps
        self.sibling = [(i, i ^ 1) for i in range(devices)]
        at = [(j, core) for j in range(self.chips) for core in (0, 1)]
        self.first_at, self.late_at = at[: self.EARLY], at[self.EARLY :]

    def owner(self, device, distance, core):
        return 2 * ((device // 2 + distance) % self.chips) + (device % 2 + core) % 2

    def shift(self, step):
        return [(i, (i + 2 * step) % self.devices) for i in range(self.devices)]

    def gather(self, block, device):
        tokens, width = block.shape
        whole = jnp.zeros((tokens, width * self.devices), block.dtype)

        def put(whole, part, distance):
            whole = place(whole, part, self.owner(device, distance, 0))
            other = lax.ppermute(part, "fsdp", self.sibling)
            return place(whole, other, self.owner(device, distance, 1))

        whole = put(whole, block, 0)
        up = down = block
        for step in range(1, self.up_steps + 1):
            up = lax.ppermute(up, "fsdp", self.shift(1))
            if step <= self.down_steps:
                down = lax.ppermute(down, "fsdp", self.shift(-1))
            whole = put(whole, up, self.chips - step)
            if step <= self.down_steps:
                whole = put(whole, down, step)
        return whole, [block], block

    def scatter_sum(self, product):
        keep = product([], list(range(self.chips)), None)

        def term(distance):
            return keep[distance]

        up = term(self.up_steps)
        down = term(self.up_steps + 1) if self.down_steps else None
        for step in range(1, self.up_steps + 1):
            up = lax.ppermute(up.astype(BF16), "fsdp", self.shift(1)).astype(F32)
            if step <= self.down_steps:
                down = lax.ppermute(down.astype(BF16), "fsdp", self.shift(-1)).astype(F32)
            if step < self.up_steps:
                up = up + term(self.up_steps - step)
            if step < self.down_steps:
                down = down + term(self.up_steps + 1 + step)
        total = term(0) + up
        return (total + down if self.down_steps else total), keep[0]


class Grid(Ring):
    FAR_FIRST = (3, 2, 1, 0)
    EARLY = 14

    def across(self, bits):
        return [(i, i ^ bits) for i in range(self.devices)]

    def owner(self, device, distance, core):
        return jnp.bitwise_xor(device, 2 * distance + core)

    def gather(self, block, device):
        first = []
        tokens, width = block.shape
        whole = jnp.zeros((tokens, width * self.devices), block.dtype)
        column = {0: block}
        for z in (1, 2):
            column[z] = lax.ppermute(block, "fsdp", self.across(4 * z))
        column[3] = lax.ppermute(after(block, column[1]), "fsdp", self.across(12))
        for z in range(4):
            for y in range(2):
                part = lax.ppermute(column[z], "fsdp", self.across(2)) if y else column[z]
                whole = place(whole, part, self.owner(device, 2 * z + y, 0))
                other = lax.ppermute(part, "fsdp", self.sibling)
                whole = place(whole, other, self.owner(device, 2 * z + y, 1))
                if 2 * z + y < 7:
                    first += [part, other]
        return whole, first, column[1]

    def scatter_sum(self, product):
        over_y = {}
        mine = {}
        sent = None
        for z in self.FAR_FIRST:
            sent, mine[z] = product([2 * z + 1], [2 * z], sent)
            over_y[z] = lax.ppermute(sent, "fsdp", self.across(2))
        arrived = []
        sent = None
        for z in self.FAR_FIRST:
            part = over_y[z] if sent is None else after(over_y[z], sent)
            total = mine[z] + part.astype(F32)
            if z:
                sent = total.astype(BF16)
                arrived.append(lax.ppermute(sent, "fsdp", self.across(4 * z)))
        for part in arrived:
            total = total + part.astype(F32)
        return total, sent


def kept_rows(kept_index, device, parent_rows):
    local = kept_index[:, None] - device * parent_rows
    kept = jnp.any(local == jnp.arange(parent_rows)[None, :], axis=0)
    return kept.astype(F32).reshape(1, parent_rows)


def routing(kept_index, tile_owner, device, devices, parent_rows, stride):
    tile_count = tile_owner.shape[0]
    tile_rows = kept_index.shape[0] // tile_count
    slots = devices * stride
    layout = kept_index.reshape(tile_count, tile_rows)
    local = layout - device * parent_rows
    mine = (local >= 0) & (local < parent_rows)
    earlier = jnp.arange(tile_rows)[:, None] < jnp.arange(tile_rows)[None, :]
    position = dot(mine.astype(BF16), earlier.astype(BF16)).astype(jnp.int32)
    slot = jnp.where(mine, tile_owner[:, None] * stride + position, -1).reshape(-1)
    at_slot = (slot[None, :] == jnp.arange(slots)[:, None]).astype(BF16)
    at_row = (local.reshape(-1)[:, None] == jnp.arange(parent_rows)[None, :]).astype(BF16)
    send = dot(at_slot, at_row).astype(BF16)
    tile = jnp.sum(jnp.where((tile_owner == device)[:, None], layout, 0), axis=0)
    source = jnp.where(tile >= 0, tile // parent_rows, -1)
    same = (source[:, None] == source[None, :]) & earlier.T
    rank = jnp.sum(same.astype(jnp.int32), axis=1)
    slot = jnp.where(tile >= 0, source * stride + rank, -slots)
    find = (slot[:, None] == jnp.arange(slots)[None, :]).astype(BF16)
    return send, find


def squares_kernel(*refs):
    blocks, squares = refs[:-1], refs[-1]
    total = jnp.zeros(blocks[0].shape, F32)
    for block in blocks:
        h = block[...].astype(F32)
        total = total + h * h
    squares[...] = jnp.broadcast_to(jnp.sum(total, axis=1, keepdims=True), squares.shape)


def forward_kernel(
    ring, early, hidden, parent_gain, child_gain, gate, up, kept, scale, child_gate, child_up, both_hid
):
    tokens, features = hidden.shape
    pieces = 16
    piece = features // pieces
    cuts = [slice(k * piece, (k + 1) * piece) for k in range(pieces)]
    width = features // ring.devices
    device = lax.axis_index("fsdp")
    squares = jnp.zeros((tokens, width), F32)
    for at in ring.late_at:
        start = ring.owner(device, *at) * width
        h = hidden[:, pl.ds(pl.multiple_of(start, width), width)].astype(F32)
        squares = squares + h * h
    mean = (early[...][:, :1] + jnp.sum(squares, axis=1, keepdims=True)) / features
    inverse = 1.0 / jnp.sqrt(mean + 1e-05)
    scale[...] = jnp.broadcast_to(inverse, scale.shape)
    rows = gate.shape[0]
    products = jnp.zeros((2 * tokens, 2 * rows), F32)
    for cols in cuts:
        normed = hidden[:, cols].astype(F32) * inverse
        parent = (normed * parent_gain[:, cols]).astype(BF16)
        child = (normed * child_gain[:, cols]).astype(BF16)
        both = jnp.concatenate([parent, child], axis=0)
        weights = jnp.concatenate([gate[:, cols], up[:, cols]], axis=0)
        products = products + dot_nt(both, weights)
    gate_both, up_both = products[:, :rows], products[:, rows:]
    hid = gate_both * jax.nn.sigmoid(gate_both) * up_both
    child_gate[...] = gate_both[tokens:]
    child_up[...] = up_both[tokens:]
    child = jnp.where(kept[...] > 0, hid[tokens:], 0.0).astype(BF16)
    both_hid[:tokens, :] = child
    both_hid[tokens:, :] = -hid[:tokens].astype(BF16)


def difference_kernel(ring, distances, hid, other_hid, down, other_down, *parts):
    tokens = hid.shape[0] // 2
    width = down.shape[1] // ring.devices
    device = lax.axis_index("fsdp")
    left = jnp.concatenate([hid[...], other_hid[...]], axis=1)
    for distance, part in zip(distances, parts):
        start = ring.owner(device, distance, 0) * width
        cols = pl.ds(pl.multiple_of(start, width), width)
        right = jnp.concatenate([down[:, cols], other_down[:, cols]], axis=0)
        out = dot(left, right)
        part[...] = (out[:tokens] + out[tokens:]).astype(part.dtype)


def early_kernel(ring, *refs):
    blocks, (down, partial) = refs[:-2], refs[-2:]
    tokens, width = blocks[0].shape
    device = lax.axis_index("fsdp")
    total = jnp.zeros(partial.shape, F32)
    for block, at in zip(blocks, ring.first_at):
        start = ring.owner(device, *at) * width
        cols = pl.ds(pl.multiple_of(start, width), width)
        total = total + dot_nt(block[...], down[:, cols])
    partial[...] = total


def backward_kernel(
    per_pair,
    ring,
    partial,
    slope,
    hidden,
    gate,
    up,
    down,
    kept,
    scale,
    child_gate,
    child_up,
    both_hid,
    select,
    sent,
    message,
):
    devices, stride, _ = message.shape
    tokens = slope.shape[0]
    width = slope.shape[1] // devices
    device = lax.axis_index("fsdp")
    child_slope = partial[...]
    for at in ring.late_at:
        start = ring.owner(device, *at) * width
        cols = pl.ds(pl.multiple_of(start, width), width)
        child_slope = child_slope + dot_nt(slope[:, cols], down[:, cols])
    g, u = child_gate[...], child_up[...]
    sig = jax.nn.sigmoid(g)
    live = kept[...] > 0
    gate_back = child_slope * u * sig * (1.0 + g * (1.0 - sig))
    gate_back = jnp.where(live, gate_back, 0.0).astype(BF16)
    up_back = jnp.where(live, child_slope * g * sig, 0.0).astype(BF16)
    rows = dot_nt(select[0], gate_back) + dot_nt(select[1], up_back)
    rows = rows + dot_nt(select[2], both_hid[:tokens, :])
    message[...] = rows.reshape(devices, stride, tokens)
    both_back = jnp.concatenate([gate_back, up_back], axis=1)
    inverse = scale[...][:, :1]
    high_at, gain_rows = 3 * per_pair, width // 128
    for k in range(devices):
        cols = slice(k * width, (k + 1) * width)
        weights = jnp.concatenate([gate[:, cols], up[:, cols]], axis=0)
        input_slope = dot(both_back, weights)
        normed = hidden[:, cols].astype(F32) * inverse
        part = jnp.sum(input_slope * normed, axis=0, keepdims=True)
        high = part.astype(BF16).astype(F32)
        for r in range(gain_rows):
            lanes = slice(r * 128, (r + 1) * 128)
            at = high_at + r
            message[k, at : at + 1, :] = high[:, lanes]
            at = at + gain_rows
            message[k, at : at + 1, :] = (part - high)[:, lanes]
    sent[...] = message[...].astype(BF16)


def prepare_kernel(hidden, scale, child_gain, slope, child_in, loss):
    tokens, features = hidden.shape
    inverse = scale[...][:, :1]
    cut = min(features, 512)
    squares = jnp.zeros((tokens, cut), F32)
    for k in range(features // cut):
        cols = slice(k * cut, (k + 1) * cut)
        difference = slope[:, cols].astype(F32)
        squares = squares + difference * difference
        child = hidden[:, cols].astype(F32) * inverse * child_gain[:, cols]
        child_in[:, cols] = child.astype(BF16)
    squares = jnp.sum(jnp.sum(squares, axis=0, keepdims=True), axis=1, keepdims=True)
    loss[...] = 0.5 * squares / (tokens * features)


def write_rows(tile, source, grads, made, done):
    rows, features = grads[0].shape
    cut = min(features, 1024)
    copies = []
    for k in range(features // cut):
        cols = slice(k * cut, (k + 1) * cut)
        out = dot(tile, source[:, cols]).astype(BF16)
        for kind, grad in enumerate(grads):
            made[kind, :, cols] = out[kind * rows : (kind + 1) * rows]
            copy = pltpu.make_async_copy(made.at[kind, :, cols], grad.at[:, cols], done.at[kind, k])
            copy.start()
            copies.append(copy)
    return copies


def down_kernel(per_pair, received, places, slope, grad_down, gain, made, done):
    devices, stride, tokens = received.shape
    message = received[...].reshape(devices * stride, tokens)
    tile = dot(places[2], message).astype(BF16)
    copies = write_rows(tile, slope, [grad_down], made, done)
    total = jnp.sum(message.astype(F32).reshape(devices, stride, tokens), axis=0)
    gain_rows = gain.shape[1] // 128
    for r in range(gain_rows):
        at = 3 * per_pair + r
        gain[:, r * 128 : (r + 1) * 128] = (
            total[at : at + 1, :] + total[at + gain_rows : at + gain_rows + 1, :]
        )
    for copy in copies:
        copy.wait()


def rows_kernel(received, places, child_in, grad_gate, grad_up, made, done):
    devices, stride, tokens = received.shape
    message = received[...].reshape(devices * stride, tokens)
    tiles = [dot(places[kind], message).astype(BF16) for kind in range(2)]
    both = jnp.concatenate(tiles, axis=0)
    for copy in write_rows(both, child_in, [grad_gate, grad_up], made, done):
        copy.wait()


VMEM = pl.BlockSpec(memory_space=pltpu.VMEM)
MIB = 1024 * 1024


def call(kernel, outs, operands, limit, name, scratch=(), specs=None):
    return pl.pallas_call(
        kernel,
        out_shape=[jax.ShapeDtypeStruct(shape, dtype) for shape, dtype in outs],
        in_specs=[VMEM] * len(operands),
        out_specs=specs or [VMEM] * len(outs),
        scratch_shapes=list(scratch),
        compiler_params=pltpu.CompilerParams(vmem_limit_bytes=limit * MIB),
        name=name,
    )(*operands)


def shards(
    hidden, parent_gain, child_gain, gate_weight, up_weight, down_weight, kept_index, tile_owner
):
    devices = lax.axis_size("fsdp")
    device = lax.axis_index("fsdp")
    ring = Grid(devices) if devices == 16 else Ring(devices)
    chips = ring.chips
    parent_rows = gate_weight.shape[0]
    tokens, width = hidden.shape
    features = width * devices
    per_pair = kept_index.shape[0] // tile_owner.shape[0] // devices
    stride = -(-(3 * per_pair + 2 * (width // 128)) // 8) * 8
    square = ((tokens, parent_rows), F32)
    gains = [parent_gain.reshape(1, features), child_gain.reshape(1, features)]
    hidden_all, first, early = ring.gather(hidden, device)
    kept = kept_rows(after(kept_index, early), device, parent_rows)
    (early_squares,) = call(
        squares_kernel, [((tokens, 128), F32)], first, limit=6, name="squares"
    )
    scale, child_gate, child_up, both_hid = call(
        functools.partial(forward_kernel, ring),
        [((tokens, 128), F32), square, square, ((2 * tokens, parent_rows), BF16)],
        [early_squares, hidden_all, *gains, gate_weight, up_weight, kept],
        limit=6,
        name="forward",
    )
    other_down = lax.ppermute(down_weight, "fsdp", ring.sibling)
    other_hid = lax.ppermute(both_hid, "fsdp", ring.sibling)

    def product(rounded, exact, previous):
        block = (tokens, width)
        hid = both_hid if previous is None else after(both_hid, previous)
        return call(
            functools.partial(difference_kernel, ring, rounded + exact),
            [(block, BF16)] * len(rounded) + [(block, F32)] * len(exact),
            [hid, other_hid, down_weight, other_down],
            limit=6,
            name="difference",
        )

    difference, last_sent = ring.scatter_sum(product)
    slope_all, first_slope, _ = ring.gather(difference.astype(BF16), device)

    kept_index, tile_owner, _ = lax.optimization_barrier((kept_index, tile_owner, last_sent))
    send, find = routing(kept_index, tile_owner, device, devices, parent_rows, stride)
    select = jnp.stack([jnp.roll(send, kind * per_pair, axis=0) for kind in range(3)])
    places = jnp.stack([jnp.roll(find, kind * per_pair, axis=1) for kind in range(3)])
    message = (devices, stride, tokens)
    (partial,) = call(
        functools.partial(early_kernel, ring),
        [square],
        [*first_slope, down_weight],
        limit=6,
        name="early",
    )
    (sent,) = call(
        functools.partial(backward_kernel, per_pair, ring),
        [(message, BF16)],
        [
            partial,
            slope_all,
            hidden_all,
            gate_weight,
            up_weight,
            down_weight,
            kept,
            scale,
            child_gate,
            child_up,
            both_hid,
            select,
        ],
        limit=6,
        name="backward",
        scratch=[pltpu.VMEM(message, F32)],
    )
    received = lax.all_to_all(sent, "fsdp", 0, 0, tiled=True)
    anywhere = pl.BlockSpec(memory_space=pl.ANY)
    grad = ((parent_rows, features), BF16)
    child_in, loss_value = call(
        prepare_kernel,
        [((tokens, features), BF16), ((1, 1), F32)],
        [after(hidden_all, sent), scale, gains[1], slope_all],
        limit=6,
        name="prepare",
    )
    cuts = features // min(features, 1024)
    grad_down, gain_grad = call(
        functools.partial(down_kernel, per_pair),
        [grad, ((1, width), F32)],
        [received, places, slope_all],
        limit=6,
        name="down",
        scratch=[
            pltpu.VMEM((1, parent_rows, features), BF16),
            pltpu.SemaphoreType.DMA((1, cuts)),
        ],
        specs=[anywhere, VMEM],
    )
    grad_gate, grad_up = call(
        rows_kernel,
        [grad, grad],
        [after(received, gain_grad), places, child_in],
        limit=8,
        name="rows",
        scratch=[
            pltpu.VMEM((2, parent_rows, features), BF16),
            pltpu.SemaphoreType.DMA((2, cuts)),
        ],
        specs=[anywhere] * 2,
    )
    return (grad_gate, grad_up, grad_down, gain_grad.reshape(width), loss_value.reshape(1))


def solution(mesh):
    placed = (
        P("groups", "fsdp"),
        P("groups"),
        P("groups"),
        P(("groups", "fsdp"), None),
        P(("groups", "fsdp"), None),
        P(("groups", "fsdp"), None),
        P("groups"),
        P("groups"),
    )
    return jax.shard_map(
        shards,
        mesh=mesh,
        in_specs=placed,
        out_specs=(
            P(("groups", "fsdp"), None),
            P(("groups", "fsdp"), None),
            P(("groups", "fsdp"), None),
            P(("groups", "fsdp")),
            P("groups"),
        ),
        check_vma=False,
    )
```
